512 devices in a mesh: cell: 32 (over z, core), rays: 16 (over y, x).
Axes of the slice: x: 4, y: 4, z: 16, core: 2. Of those that a mesh axis runs over, the one named last changes fastest.
Arguments:
- ray_code: bfloat16 [4096, 32, 256], P('rays', 'cell'), may hold values from -6 to 6
- entry_index: int32 [4096, 32], P('rays', 'cell'), may hold values from 0 to 120
- sample_count: int32 [4096, 32], P('rays', 'cell'), may hold values from 0 to 8
- step_length: float32 [4096, 32], P('rays', 'cell'), may hold values from 0.0001 to 0.75
- positions: bfloat16 [32, 128, 256], P('cell'), may hold values from -6 to 6
- w_first: bfloat16 [32, 256, 256], P('cell'), may hold values from -0.375 to 0.375
- w_second: float32 [32, 256, 256], P('cell'), may hold values from -0.375 to 0.375
- w_density: bfloat16 [32, 256], P('cell'), may hold values from -0.375 to 0.375
- w_feature: float32 [32, 256, 768], P('cell'), may hold values from -0.375 to 0.375
- mean_second: float32 [32, 256, 256], P('cell'), may hold values from -2 to 2
- square_second: float32 [32, 256, 256], P('cell'), may hold values from 0.0005 to 0.002
- mean_feature: float32 [32, 256, 768], P('cell'), may hold values from -2 to 2
- square_feature: float32 [32, 256, 768], P('cell'), may hold values from 0.0005 to 0.002
- target_color: bfloat16 [4096, 768], P('rays'), may hold values from -6 to 6
Outputs:
- rendered: bfloat16 [4096, 768], P('rays', 'cell')
- depth_grad: float32 [4096, 32], P('rays', 'cell')
- update_second: bfloat16 [32, 256, 256], P('cell')
- update_feature: bfloat16 [32, 256, 768], P('cell')
The draws below stay inside these ranges and needn't reach their ends.
Inputs may be any that keep to these rules, and one draw needn't show every extreme that they name: Samples of a ray in a cell use the table rows entry_index to entry_index + 7. Slots from sample_count on lie outside the cell.
All inputs are finite; a program needn't handle non-finite values.
Results may differ from the reference program's by a relative error of at most 0.0075.
Values may be sent and summed in bfloat16 or wider, within the bound.
A program may use at most 64 MiB of HBM per device.

```python
import math
import jax
import jax.numpy as jnp
from jax import lax

W = 256
F = 768
SAMPLES = 8
POSITIONS = 128
REGION_COUNT = 32
BEAM_COUNT = 4096


def draw_step_length(key, part):
    stochastic_seeds = jax.random.split(jax.random.fold_in(key, 17), 4)
    low_rate, high_rate = (math.log(0.0003), math.log(0.3))
    beam_proportion = jnp.exp(jax.random.uniform(stochastic_seeds[0], (BEAM_COUNT, 1), jnp.float32, low_rate, high_rate))
    approximate_guess = jnp.exp(jax.random.uniform(stochastic_seeds[1], (BEAM_COUNT, REGION_COUNT), jnp.float32, math.log(0.5), math.log(2.0)))
    sample_batch = jax.random.uniform(stochastic_seeds[2], (BEAM_COUNT, REGION_COUNT), jnp.float32) < 0.08
    additional_summand = jax.random.uniform(stochastic_seeds[3], (BEAM_COUNT, REGION_COUNT), jnp.float32, 0.04, 0.12)
    return beam_proportion * approximate_guess + jnp.where(sample_batch, additional_summand, 0.0)


def draw_target_color(key, part):
    color_seeds = jax.random.split(jax.random.fold_in(key, 29), 1)
    teacher = jax.random.normal(color_seeds[0], (BEAM_COUNT, F), jnp.float32)
    return jnp.clip(teacher, -6.0, 6.0).astype(jnp.bfloat16)


def touch_ends(drawn, key, low, high):
    spot = [jax.random.randint(jax.random.fold_in(key, axis), (), 0, length) for axis, length in enumerate(drawn.shape)]
    widest = drawn.shape.index(max(drawn.shape))
    next_to = spot[:widest] + [(spot[widest] + 1) % drawn.shape[widest]] + spot[widest + 1:]
    return drawn.at[tuple(spot)].set(low).at[tuple(next_to)].set(high)


def steps_of(stream_key, dims, cuts, low, top_value):
    def one(axis_at, parts):
        heights = jax.random.uniform(jax.random.fold_in(jax.random.fold_in(stream_key, 6), axis_at), (parts,), jnp.float32, low / len(cuts), top_value / len(cuts))
        return jnp.repeat(jnp.exp(heights), dims[axis_at] // parts).reshape((-1,) + (1,) * (len(dims) - axis_at - 1))

    level = one(*cuts[0])
    for cut in cuts[1:]:
        level = level * one(*cut)
    return level


def noise(stream_key, shape, deviation, limit, cuts=(), kind=jnp.bfloat16):
    result = deviation * jax.random.normal(stream_key, shape, jnp.float32)
    if cuts:
        result = result * steps_of(stream_key, shape, cuts, -0.22, 0.18)
    return jnp.clip(result, -limit, limit).astype(kind)


def setup_inputs(seed: int = 0) -> dict:
    key_of = jax.random.split(jax.random.key(seed), 15)
    return {
        "ray_code": noise(key_of[0], (BEAM_COUNT, REGION_COUNT, W), 1.0, 6.0, ((0, 16), (1, 32))),
        "entry_index": touch_ends(jax.random.randint(key_of[1], (BEAM_COUNT, REGION_COUNT), 0, POSITIONS - SAMPLES + 1), jax.random.fold_in(key_of[1], 1), 0, POSITIONS - SAMPLES).astype(jnp.int32),
        "sample_count": touch_ends(jax.random.randint(key_of[2], (BEAM_COUNT, REGION_COUNT), 0, SAMPLES + 1), jax.random.fold_in(key_of[2], 1), 0, SAMPLES).astype(jnp.int32),
        "step_length": draw_step_length(jax.random.fold_in(key_of[14], 71), 0),
        "positions": noise(key_of[4], (REGION_COUNT, POSITIONS, W), 1.0, 6.0, ((0, 32),)),
        "w_first": noise(key_of[5], (REGION_COUNT, W, W), W ** -0.5, 0.375, ((0, 32),)),
        "w_second": noise(key_of[6], (REGION_COUNT, W, W), W ** -0.5, 0.375, ((0, 32),), jnp.float32),
        "w_density": noise(key_of[7], (REGION_COUNT, W), W ** -0.5, 0.375, ((0, 32),)),
        "w_feature": noise(key_of[8], (REGION_COUNT, W, F), W ** -0.5, 0.375, ((0, 32),), jnp.float32),
        "mean_second": noise(key_of[9], (REGION_COUNT, W, W), 0.3, 2.0, ((0, 32),), jnp.float32),
        "square_second": jnp.clip(jnp.exp(math.log(0.002) - 1.3862944 * jax.random.uniform(key_of[10], (REGION_COUNT, W, W), jnp.float32) ** steps_of(key_of[10], (REGION_COUNT, W, W), ((0, 32),), -0.2, 0.2)), 0.0005, 0.002),
        "mean_feature": noise(key_of[11], (REGION_COUNT, W, F), 0.3, 2.0, ((0, 32),), jnp.float32),
        "square_feature": jnp.clip(jnp.exp(math.log(0.002) - 1.3862944 * jax.random.uniform(key_of[12], (REGION_COUNT, W, F), jnp.float32) ** steps_of(key_of[12], (REGION_COUNT, W, F), ((0, 32),), -0.2, 0.2)), 0.0005, 0.002),
        "target_color": draw_target_color(jax.random.fold_in(key_of[14], 71), 0),
    }


beta_first = 0.9
beta_second = 0.999
bias_first = 0.19
bias_second = 0.001999
adam_floor = 1e-08
mean_floor = 1e-06

def cell_forward(ray_feat, place_table, entry_index, sample_count, step_length, w_first, w_second, w_density, w_feature):
    ray_rows = ray_feat.shape[0]
    offsets = jnp.arange(SAMPLES, dtype=jnp.int32)
    sample_spot = entry_index[:, None].astype(jnp.int32) + offsets[None, :]
    table_slot = jnp.arange(place_table.shape[0], dtype=jnp.int32)
    one_hot = (sample_spot.reshape(-1, 1) == table_slot[None, :]).astype(jnp.bfloat16)
    placed = jnp.dot(one_hot, place_table, preferred_element_type=jnp.float32)
    inputs = (placed.reshape(ray_rows, SAMPLES, -1) + ray_feat[:, None, :].astype(jnp.float32)).astype(jnp.bfloat16)
    inputs = inputs.reshape(ray_rows * SAMPLES, -1)
    hidden_one = jax.nn.relu(jnp.dot(inputs, w_first, preferred_element_type=jnp.float32)).astype(jnp.bfloat16)
    before = jnp.dot(hidden_one, w_second.astype(jnp.bfloat16), preferred_element_type=jnp.float32)
    hidden_two = jax.nn.relu(before).astype(jnp.bfloat16)
    feature = jnp.dot(hidden_two, w_feature.astype(jnp.bfloat16), preferred_element_type=jnp.float32)
    density_logit = jnp.dot(hidden_two, w_density, preferred_element_type=jnp.float32)
    inside = (offsets[None, :] < sample_count[:, None]).astype(jnp.float32)
    travel = step_length[:, None] * inside
    depth_step = jax.nn.softplus(density_logit).reshape(ray_rows, SAMPLES) * travel
    return (hidden_one, before, hidden_two, feature, density_logit, travel, depth_step)

def composite(depth_step, feature_cube):
    ahead_depth = jnp.cumsum(depth_step, axis=1) - depth_step
    weight = jnp.exp(-ahead_depth) * (1.0 - jnp.exp(-depth_step))
    partial_value = jnp.einsum('rs,rsf->rf', weight, feature_cube)
    return (partial_value, lax.optimization_barrier(jnp.sum(depth_step, axis=1)))

def cell_backward(stored, w_density, w_feature, grad_part, grad_depth):
    hidden_one, before, hidden_two, feature, density_logit, travel, depth_step = stored
    ray_rows = depth_step.shape[0]
    feature_cube = feature.reshape(ray_rows, SAMPLES, -1)
    _, pullback = jax.vjp(composite, depth_step, feature_cube)
    grad_step, grad_cube = pullback((grad_part, grad_depth))
    grad_rows = grad_cube.reshape(ray_rows * SAMPLES, -1).astype(jnp.bfloat16)
    grad_feature = jnp.dot(hidden_two.T, grad_rows, preferred_element_type=jnp.float32)
    grad_logit = (grad_step * travel).reshape(-1) * jax.nn.sigmoid(density_logit)
    grad_hidden = jnp.dot(grad_rows, w_feature.astype(jnp.bfloat16).T, preferred_element_type=jnp.float32)
    grad_hidden = grad_hidden + grad_logit[:, None] * w_density.astype(jnp.float32)[None, :]
    grad_before = jnp.where(before > 0, grad_hidden, 0.0).astype(jnp.bfloat16)
    grad_second = jnp.dot(hidden_one.T, grad_before, preferred_element_type=jnp.float32)
    return (grad_second, grad_feature)

def adam_update(gradient, mean_moment, square_moment, rescale):
    unit_grad = gradient * rescale
    mean_new = beta_first * mean_moment + (1.0 - beta_first) * unit_grad
    square_new = beta_second * square_moment + (1.0 - beta_second) * unit_grad * unit_grad
    return (mean_new / bias_first / (jnp.sqrt(square_new / bias_second) + adam_floor)).astype(jnp.bfloat16)

def reference(ray_code, entry_index, sample_count, step_length, positions, w_first, w_second, w_density, w_feature, mean_second, square_second, mean_feature, square_feature, target_color):
    per_cell = (jnp.swapaxes(ray_code, 0, 1), positions, entry_index.T, sample_count.T, step_length.T, w_first, w_second, w_density, w_feature)

    def forward(cell_items):
        stored = cell_forward(cell_items[0], cell_items[1], cell_items[2], cell_items[3], cell_items[4], cell_items[5], cell_items[6], cell_items[7], cell_items[8])
        ray_rows = cell_items[0].shape[0]
        return composite(stored[6], stored[3].reshape(ray_rows, SAMPLES, -1))
    partials, depths = lax.map(forward, per_cell)
    ahead_depth = jnp.cumsum(depths, axis=0) - depths
    transmit = jnp.exp(-ahead_depth)
    composite_full = lax.optimization_barrier(jnp.sum(transmit[:, :, None] * partials, axis=0))
    residual = composite_full - target_color.astype(jnp.float32)
    bright = transmit * lax.optimization_barrier(jnp.sum(partials * residual[None], axis=2))
    later_sum = lax.optimization_barrier(jnp.sum(bright, axis=0))[None] - jnp.cumsum(bright, axis=0)
    grad_parts = transmit[:, :, None] * residual[None]

    def backward(cell_items):
        stored = cell_forward(cell_items[0], cell_items[1], cell_items[2], cell_items[3], cell_items[4], cell_items[5], cell_items[6], cell_items[7], cell_items[8])
        return cell_backward(stored, cell_items[7], cell_items[8], cell_items[9], -cell_items[10])
    grads_second, grads_feature = lax.map(backward, per_cell + (grad_parts, later_sum))
    square_sum = jnp.sum(grads_second * grads_second) + jnp.sum(grads_feature * grads_feature)
    entry_total = grads_second.size + grads_feature.size
    rescale = lax.rsqrt(square_sum / entry_total + mean_floor)
    update_second = adam_update(grads_second, mean_second, square_second, rescale)
    update_feature = adam_update(grads_feature, mean_feature, square_feature, rescale)
    depth_grad = -later_sum.T
    return (composite_full.astype(jnp.bfloat16), depth_grad, update_second, update_feature)
```

```python
import functools

import jax
import jax.numpy as jnp
from jax import lax
from jax.experimental import pallas as pl
from jax.experimental.pallas import tpu as pltpu
from jax.sharding import Mesh
from jax.sharding import PartitionSpec as P

SAMPLES = 8
MESH = pl.DeviceIdType.MESH
CELL = ("z", "core")
RAYS = ("y", "x")
HALF = 128
F32 = jnp.float32
BF16 = jnp.bfloat16

beta_first = 0.9
beta_second = 0.999
bias_first = 0.19
bias_second = 0.001999
adam_floor = 1e-08
mean_floor = 1e-06


def nt_dot(a, b):
    return lax.dot_general(a, b, (((1,), (1,)), ((), ())), preferred_element_type=F32)


def mm(a, b):
    return jnp.dot(a, b, preferred_element_type=F32)


def kernel(
    sizes,
    ray_h, ent_h, cnt_h, stp_h, pos_h, w1_h, w2_h, wd_h, wf_h,
    ms_h, vs_h, mf_h, vf_h, tgt_h,
    ren_o, dg_o, us_o, uf_o,
    ray_v, ent_v, cnt_v, stp_v, pos_v, w1_v, w2_v, wd_v, wf_v,
    ms_v, vs_v, mf_v, vf_v, tgt_v,
    rayt, post, w1t, w2t, wft, wfb, wdb, h1, h2, lg, tgt_t, q_t, gp,
    dep, tt, pl_s, pr_s, ns_s, nr_s, fs_s, fr_s, cp_s, cr_s, rs_s, br,
    gf_s, gf_r, gs_s, gs_r, ga, sq, sr,
    loc, many_send, many_recv, one_send, one_recv,
):
    n_z, n_y, n_x, all_cells = sizes
    n_cell, n_rays = 2 * n_z, n_y * n_x
    z, core = lax.axis_index("z"), lax.axis_index("core")
    y, x = lax.axis_index("y"), lax.axis_index("x")
    cell = 2 * z + core
    group = n_x * y + x
    quad, res = lax.div(z, 4), lax.rem(z, 4)
    other = 1 - core

    def cell_device(t):
        return (lax.div(t, 2), lax.rem(t, 2), y, x)

    def rays_device(t):
        return (z, core, lax.div(t, n_x), lax.rem(t, n_x))

    def chip_device(t):
        return (lax.rem(t + n_z, n_z), core, y, x)

    sibling = (z, other, y, x)

    def each_cell(send):
        lax.fori_loop(1, n_cell, lambda j, n: (send(lax.rem(cell + j, n_cell)), n)[1], 0)

    def each_group(send):
        def step(j, n):
            to_y = lax.rem(y + lax.div(j, n_x), n_y)
            to_x = lax.rem(x + lax.rem(j, n_x), n_x)
            send(to_y * n_x + to_x)
            return n

        lax.fori_loop(1, n_rays, step, 0)

    bring = {}
    for i, (name, src, dst) in enumerate((
        ("ent", ent_h, ent_v), ("pos", pos_h, pos_v), ("ray", ray_h, ray_v), ("w1", w1_h, w1_v),
        ("w2", w2_h, w2_v), ("wd", wd_h, wd_v), ("cnt", cnt_h, cnt_v), ("stp", stp_h, stp_v),
        ("wf", wf_h, wf_v),
        ("tgt", tgt_h.at[pl.ds(pl.multiple_of(core * HALF, HALF), HALF), :], tgt_v),
        ("ms", ms_h, ms_v), ("vs", vs_h, vs_v), ("mf", mf_h, mf_v), ("vf", vf_h, vf_v),
    )):
        bring[name] = pltpu.make_async_copy(src, dst, loc.at[i])
        bring[name].start()

    barrier = pltpu.get_barrier_semaphore()
    each_cell(lambda t: pl.semaphore_signal(barrier, inc=1, device_id=cell_device(t), device_id_type=MESH))
    each_group(lambda t: pl.semaphore_signal(barrier, inc=1, device_id=rays_device(t), device_id_type=MESH))

    for name in ("ent", "pos", "ray", "w1"):
        bring[name].wait()
    post[...] = pos_v[...].astype(F32).T.astype(BF16)
    rayt[...] = ray_v[...].astype(F32).T
    w1t[...] = w1_v[...].astype(F32).T.astype(BF16)
    for name in ("w2", "wd", "cnt", "stp"):
        bring[name].wait()
    w2t[...] = w2_v[...].T.astype(BF16)
    width = wd_v.shape[1]
    n_rows = ray_v.shape[0]
    wdb[...] = jnp.broadcast_to(wd_v[...].astype(F32), (n_rows, width)).T
    slot = lax.broadcasted_iota(jnp.int32, (pos_v.shape[0], n_rows), 0)

    def forward(k):
        hot = jnp.where(slot == ent_v[...] + k, 1.0, 0.0).astype(BF16)
        inputs = (mm(post[...], hot) + rayt[...]).astype(BF16)
        first = jnp.maximum(mm(w1t[...], inputs), 0.0).astype(BF16)
        second = jnp.maximum(mm(w2t[...], first), 0.0).astype(BF16)
        h1[k] = first
        h2[k] = second
        lg[pl.ds(k, 1), :] = jnp.sum(second.astype(F32) * wdb[...], axis=0, keepdims=True)

    def two(i, n):
        forward(2 * i)
        forward(2 * i + 1)
        return n

    lax.fori_loop(0, SAMPLES // 2, two, 0)

    order = lax.broadcasted_iota(jnp.int32, (SAMPLES, n_rows), 0)
    logit = lg[...]
    travel = jnp.where(order < cnt_v[...], stp_v[...], 0.0)
    step_depth = (jnp.maximum(logit, 0.0) + jnp.log1p(jnp.exp(-jnp.abs(logit)))) * travel

    def ahead_of(v):
        total = v
        for shift in (1, 2, 4):
            total = total + jnp.where(order >= shift, pltpu.roll(total, shift, 0), 0.0)
        return total - v

    ahead = jnp.exp(-ahead_of(step_depth))
    kept = jnp.exp(-step_depth)
    weight = ahead * (1.0 - kept)
    depth = jnp.sum(step_depth, axis=0, keepdims=True)

    def put_rows(buf, at, row):
        for half in range(2):
            buf[at, pl.ds(half, 1), :] = row[:, half * HALF:(half + 1) * HALF]

    put_rows(dep, cell, depth)
    pl.semaphore_wait(barrier, n_cell - 1 + n_rays - 1)

    def to_cells(buf, i):
        each_cell(lambda t: pltpu.make_async_remote_copy(
            buf.at[cell], buf.at[cell], many_send.at[i], many_recv.at[i],
            device_id=cell_device(t), device_id_type=MESH).start())

    def to_groups(src, dst, i):
        each_group(lambda t: pltpu.make_async_remote_copy(
            src(t), dst.at[group], many_send.at[i], many_recv.at[i],
            device_id=rays_device(t), device_id_type=MESH).start())

    def wait_many(buf, sem, i):
        part = buf.at[pl.ds(0, buf.shape[0] - 1)]
        pltpu.make_async_copy(part, part, sem.at[i]).wait()

    sent = []

    def send(src, dst, i, device):
        copy = pltpu.make_async_remote_copy(
            src, dst, one_send.at[i], one_recv.at[i], device_id=device, device_id_type=MESH)
        copy.start()
        sent.append(copy)

    def arrived(dst, i):
        pltpu.make_async_copy(dst, dst, one_recv.at[i]).wait()

    to_cells(dep, 0)

    gather = weight[0:1] * h2[0].astype(F32)
    for k in range(1, SAMPLES):
        gather = gather + weight[k:k + 1] * h2[k].astype(F32)
    gathered = gather.astype(BF16)
    bring["wf"].wait()
    wfb[...] = wf_v[...].astype(BF16)
    wft[...] = wf_v[...].T.astype(BF16)
    partial = mm(wft[...], gathered).astype(BF16)
    for half in range(2):
        pl_s[half] = partial[:, half * HALF:(half + 1) * HALF].reshape(pl_s.shape[1:])
    send(pl_s.at[other], pr_s, 0, sibling)
    bring["tgt"].wait()
    tgt_t[...] = tgt_v[...].astype(F32).T.reshape(tgt_t.shape)

    wait_many(dep, many_recv, 0)
    number = lax.broadcasted_iota(jnp.int32, dep.shape, 0)
    depths = dep[...]
    before_pair = jnp.sum(jnp.where(number < 2 * z, depths, 0.0), axis=0)
    tt[0] = jnp.exp(-before_pair)
    tt[1] = jnp.exp(-(before_pair + dep[2 * z]))
    mine = tt[core, pl.ds(core, 1), :]
    theirs = tt[other, pl.ds(core, 1), :]

    arrived(pr_s, 0)
    for i in range(16):
        ns_s[i // 4, i % 4] = (mine * pl_s[core, i].astype(F32) + theirs * pr_s[i].astype(F32)).astype(BF16)

    def turn(a):
        return lax.rem(res + a + 4, 4)

    send(ns_s.at[:, turn(1)], nr_s.at[0], 1, chip_device(z + 1))
    send(ns_s.at[:, turn(-1)], nr_s.at[1], 2, chip_device(z - 1))
    send(ns_s.at[pl.ds(0, 2), turn(2)], nr_s.at[2, pl.ds(0, 2)], 3, chip_device(z + 2))
    send(ns_s.at[pl.ds(2, 2), turn(2)], nr_s.at[2, pl.ds(2, 2)], 4, chip_device(z - 2))
    arrived(nr_s.at[0], 1)
    arrived(nr_s.at[1], 2)
    arrived(nr_s.at[2, pl.ds(0, 2)], 3)
    arrived(nr_s.at[2, pl.ds(2, 2)], 4)
    for i in range(4):
        fs_s[i] = (
            ns_s[i, res].astype(F32) + nr_s[0, i].astype(F32)
            + nr_s[1, i].astype(F32) + nr_s[2, i].astype(F32)
        ).astype(BF16)
    for i in range(1, 4):
        to = lax.rem(quad + i, 4)
        send(fs_s.at[to], fr_s.at[i - 1], 4 + i, chip_device(4 * to + res))
    for i in range(1, 4):
        arrived(fr_s.at[i - 1], 4 + i)
    lit = fs_s[quad].astype(F32)
    for i in range(3):
        lit = lit + fr_s[i].astype(F32)

    rs_s[core, quad, res] = (lit - tgt_t[z]).astype(BF16)
    for i in range(1, 4):
        send(rs_s.at[core, quad, res], rs_s.at[core, quad, res], 7 + i,
             chip_device(4 * lax.rem(quad + i, 4) + res))
    cp_s[...] = lit.reshape(cp_s.shape)
    send(cp_s.at[other], cr_s, 11, sibling)
    for i in range(1, 4):
        arrived(rs_s.at[core, lax.rem(quad - i + 4, 4), res], 7 + i)
    own = rs_s.at[core, :, res]
    low, high = rs_s.at[core, pl.ds(0, 2), res], rs_s.at[core, pl.ds(2, 2), res]
    send(own, own, 12, chip_device(z + 1))
    send(own, own, 13, chip_device(z - 1))
    send(low, low, 14, chip_device(z + 2))
    send(high, high, 15, chip_device(z - 2))
    send(own, own, 16, sibling)
    came = (
        rs_s.at[core, :, turn(-1)], rs_s.at[core, :, turn(1)],
        rs_s.at[core, pl.ds(0, 2), turn(2)], rs_s.at[core, pl.ds(2, 2), turn(2)],
    )
    for i, block in enumerate(came):
        arrived(block, 12 + i)
        send(block, block, 17 + i, sibling)
    arrived(rs_s.at[other, :, res], 16)
    for i, block in enumerate((
        rs_s.at[other, :, turn(-1)], rs_s.at[other, :, turn(1)],
        rs_s.at[other, pl.ds(0, 2), turn(2)], rs_s.at[other, pl.ds(2, 2), turn(2)],
    )):
        arrived(block, 17 + i)

    transmit = tt[core]
    for half in range(2):
        block = rs_s[half].reshape(gp.shape[0], HALF).astype(F32)
        gp[:, half * HALF:(half + 1) * HALF] = (block * transmit[half:half + 1]).astype(BF16)
    q_t[...] = mm(wfb[...], gp[...])
    slopes = []
    for k in range(SAMPLES):
        slopes.append(jnp.sum(h2[k].astype(F32) * q_t[...], axis=0, keepdims=True))
    slope = jnp.concatenate(slopes, axis=0)
    lit_slope = weight * slope
    put_rows(br, cell, jnp.sum(lit_slope, axis=0, keepdims=True))
    to_cells(br, 1)
    gf_s[...] = nt_dot(gathered, gp[...]).astype(BF16).reshape(gf_s.shape)
    to_groups(lambda t: gf_s.at[t], gf_r, 2)

    arrived(cr_s, 11)
    first_half = jnp.where(core == 0, cp_s[core], cr_s[...])
    second_half = jnp.where(core == 0, cr_s[...], cp_s[core])
    ren_o[...] = jnp.concatenate([first_half, second_half], axis=1).astype(BF16)

    wait_many(br, many_recv, 1)
    later = jnp.sum(jnp.where(number > cell, br[...], 0.0), axis=0)
    grad_depth = -jnp.concatenate([later[0:1], later[1:2]], axis=1)
    dg_o[...] = grad_depth
    after = jnp.sum(lit_slope, axis=0, keepdims=True) - ahead_of(lit_slope) - lit_slope
    grad_step = grad_depth + slope * (ahead * kept) - after
    grad_logit = grad_step * travel / (1.0 + jnp.exp(-logit))
    grad_second = None
    for k in range(SAMPLES):
        grad = weight[k:k + 1] * q_t[...] + grad_logit[k:k + 1] * wdb[...]
        grad = jnp.where(h2[k].astype(F32) > 0.0, grad, 0.0).astype(BF16)
        term = nt_dot(h1[k], grad)
        grad_second = term if k == 0 else grad_second + term
    gs_s[...] = grad_second.astype(BF16).reshape(gs_s.shape)
    to_groups(lambda t: gs_s.at[t], gs_r, 3)

    gf_r[group] = gf_s[group]
    gs_r[group] = gs_s[group]
    wait_many(gf_r, many_recv, 2)
    share_feature = jnp.sum(gf_r[...].astype(F32), axis=0)
    wait_many(gs_r, many_recv, 3)
    share_second = jnp.sum(gs_r[...].astype(F32), axis=0)
    share = jnp.concatenate([share_second, share_feature], axis=1)
    squares = jnp.sum(share * share, axis=0, keepdims=True)
    folded = squares[:, 0:HALF]
    for i in range(1, squares.shape[1] // HALF):
        folded = folded + squares[:, i * HALF:(i + 1) * HALF]
    sq[cell] = folded
    to_cells(sq, 4)
    ga[group] = share.astype(BF16)
    to_groups(lambda t: ga.at[group], ga, 5)
    wait_many(sq, many_recv, 4)
    sr[group] = jnp.sum(sq[...], axis=0)
    to_groups(lambda t: sr.at[group], sr, 6)
    for name in ("ms", "vs", "mf", "vf"):
        bring[name].wait()
    wait_many(ga, many_recv, 5)
    wait_many(sr, many_recv, 6)
    square_sum = jnp.sum(jnp.sum(sr[...], axis=0), axis=1, keepdims=True)
    entry_total = all_cells * width * (width + gp.shape[0])
    rescale = lax.rsqrt(square_sum / entry_total + mean_floor)

    def adam(gradient, mean_moment, square_moment):
        unit = gradient * rescale
        mean_new = beta_first * mean_moment + (1.0 - beta_first) * unit
        square_new = beta_second * square_moment + (1.0 - beta_second) * unit * unit
        return (mean_new / bias_first / (jnp.sqrt(square_new / bias_second) + adam_floor)).astype(BF16)

    per = ga.shape[1]

    def update(i, n):
        rows = pl.ds(pl.multiple_of(i * per, per), per)
        both = ga[i].astype(F32)
        us_o[rows, :] = adam(both[:, :width], ms_v[rows, :], vs_v[rows, :])
        uf_o[rows, :] = adam(both[:, width:], mf_v[rows, :], vf_v[rows, :])
        return n

    lax.fori_loop(0, n_rays, update, 0)

    for copy in sent:
        copy.wait_send()
    for i, buf in enumerate((dep, br, gf_r, gs_r, sq, ga, sr)):
        wait_many(buf, many_send, i)


def on_device(sizes, ray_code, entry_index, sample_count, step_length, positions, w_first, w_second,
              w_density, w_feature, mean_second, square_second, mean_feature, square_feature, target_color):
    n_z, n_y, n_x, _ = sizes
    n_cell, n_rays = 2 * n_z, n_y * n_x
    rows, width = ray_code.shape[0], ray_code.shape[2]
    table, channels = positions.shape[1], target_color.shape[1]
    part = channels // 16
    per = width // n_rays
    vmem = pltpu.VMEM
    args = (
        ray_code.reshape(rows, width), entry_index.reshape(1, rows), sample_count.reshape(1, rows),
        step_length.reshape(1, rows), positions[0], w_first[0], w_second[0], w_density,
        w_feature[0], mean_second[0], square_second[0], mean_feature[0], square_feature[0], target_color,
    )
    local = [vmem(a.shape, a.dtype) for a in args[:-1]] + [vmem((HALF, channels), BF16)]
    scratch = local + [
        vmem((width, rows), F32), vmem((width, table), BF16), vmem((width, width), BF16),
        vmem((width, width), BF16), vmem((channels, width), BF16), vmem((width, channels), BF16),
        vmem((width, rows), F32), vmem((SAMPLES, width, rows), BF16), vmem((SAMPLES, width, rows), BF16),
        vmem((SAMPLES, rows), F32), vmem((16, part, HALF), F32), vmem((width, rows), F32),
        vmem((channels, rows), BF16),
        vmem((n_cell, 2, HALF), F32), vmem((2, 2, HALF), F32), vmem((2, 16, part, HALF), BF16),
        vmem((16, part, HALF), BF16), vmem((4, 4, part, HALF), BF16), vmem((3, 4, part, HALF), BF16),
        vmem((4, part, HALF), BF16), vmem((3, part, HALF), BF16), vmem((2, part // 2, HALF), F32),
        vmem((part // 2, HALF), F32), vmem((2, 4, 4, part, HALF), BF16), vmem((n_cell, 2, HALF), F32),
        vmem((n_rays, per, channels), BF16), vmem((n_rays, per, channels), BF16),
        vmem((n_rays, per, width), BF16), vmem((n_rays, per, width), BF16),
        vmem((n_rays, per, width + channels), BF16), vmem((n_cell, 1, HALF), F32), vmem((n_rays, 1, HALF), F32),
        pltpu.SemaphoreType.DMA((14,)), pltpu.SemaphoreType.DMA((7,)), pltpu.SemaphoreType.DMA((7,)),
        pltpu.SemaphoreType.DMA((21,)), pltpu.SemaphoreType.DMA((21,)),
    ]
    rendered, depth_grad, update_second, update_feature = pl.pallas_call(
        functools.partial(kernel, sizes),
        out_shape=(
            jax.ShapeDtypeStruct((part // 2, rows), BF16),
            jax.ShapeDtypeStruct((1, rows), F32),
            jax.ShapeDtypeStruct((width, width), BF16),
            jax.ShapeDtypeStruct((width, channels), BF16),
        ),
        in_specs=[pl.BlockSpec(memory_space=pl.ANY)] * len(args),
        out_specs=[pl.BlockSpec(memory_space=vmem)] * 4,
        scratch_shapes=scratch,
        compiler_params=pltpu.CompilerParams(
            collective_id=0, has_side_effects=True, vmem_limit_bytes=62 * 1024 * 1024
        ),
    )(*args)
    return (rendered.T, depth_grad.reshape(rows, 1), update_second[None], update_feature[None])


def solution(mesh):
    n_cell, n_rays = mesh.devices.shape
    n_y = 4 if n_rays == 16 else 1
    sizes = (n_cell // 2, n_y, n_rays // n_y, n_cell)
    split = Mesh(mesh.devices.reshape(n_cell // 2, 2, n_y, n_rays // n_y), ("z", "core", "y", "x"))
    return jax.shard_map(
        functools.partial(on_device, sizes),
        mesh=split,
        in_specs=(
            P(RAYS, CELL, None),
            P(RAYS, CELL),
            P(RAYS, CELL),
            P(RAYS, CELL),
            P(CELL, None, None),
            P(CELL, None, None),
            P(CELL, None, None),
            P(CELL, None),
            P(CELL, None, None),
            P(CELL, None, None),
            P(CELL, None, None),
            P(CELL, None, None),
            P(CELL, None, None),
            P(RAYS, None),
        ),
        out_specs=(P(RAYS, CELL), P(RAYS, CELL), P(CELL, None, None), P(CELL, None, None)),
        check_vma=False,
    )
```

```python
import functools

import jax
import jax.numpy as jnp
from jax import lax
from jax.experimental import pallas as pl
from jax.experimental.pallas import tpu as pltpu
from jax.sharding import Mesh
from jax.sharding import PartitionSpec as P

SAMPLES = 8
MESH = pl.DeviceIdType.MESH
CELL = ("z", "core")
RAYS = ("y", "x")
HALF = 128
F32 = jnp.float32
BF16 = jnp.bfloat16

beta_first = 0.9
beta_second = 0.999
bias_first = 0.19
bias_second = 0.001999
adam_floor = 1e-08
mean_floor = 1e-06


def nt_dot(a, b):
    return lax.dot_general(a, b, (((1,), (1,)), ((), ())), preferred_element_type=F32)


def mm(a, b):
    return jnp.dot(a, b, preferred_element_type=F32)


def kernel(
    sizes,
    ray_h, ent_h, cnt_h, stp_h, pos_h, w1_h, w2_h, wd_h, wf_h,
    tgt_h,
    ren_o, dg_o, gs_o, gf_o, sum_o,
    ray_v, ent_v, cnt_v, stp_v, pos_v, w1_v, w2_v, wd_v, wf_v,
    tgt_v,
    rayt, post, w1t, w2t, wft, wfb, wdb, h1, h2, lg, tgt_t, q_t, gp,
    dep, tt, pl_s, pr_s, ns_s, nr_s, fs_s, fr_s, cp_s, cr_s, own_s, rs_s, br,
    gf_s, gf_r, gs_s, gs_r, fa_s, sa_s, sq, sr,
    loc, many_send, many_recv, one_send, one_recv, blk_send, blk_recv,
):
    n_z, n_y, n_x, _ = sizes
    n_cell, n_rays = 2 * n_z, n_y * n_x
    z, core = lax.axis_index("z"), lax.axis_index("core")
    y, x = lax.axis_index("y"), lax.axis_index("x")
    cell = 2 * z + core
    group = n_x * y + x
    quad, res = lax.div(z, 4), lax.rem(z, 4)
    other = 1 - core

    def cell_device(t):
        return (lax.div(t, 2), lax.rem(t, 2), y, x)

    def rays_device(t):
        return (z, core, lax.div(t, n_x), lax.rem(t, n_x))

    def chip_device(t):
        return (lax.rem(t + n_z, n_z), core, y, x)

    sibling = (z, other, y, x)

    def each_cell(send):
        def step(j, n):
            to = lax.rem(z + 1 + lax.rem(lax.div(j, 2) + n_z // 2 - 2, n_z - 1), n_z)
            send(2 * to + lax.rem(j, 2))
            return n

        lax.fori_loop(0, n_cell - 2, step, 0)

    def each_group(send):
        def step(j, n):
            to_y = lax.rem(y + lax.div(j, n_x), n_y)
            to_x = lax.rem(x + lax.rem(j, n_x), n_x)
            send(to_y * n_x + to_x)
            return n

        lax.fori_loop(1, n_rays, step, 0)

    bring = {}
    for i, (name, src, dst) in enumerate((
        ("ent", ent_h, ent_v), ("pos", pos_h, pos_v), ("ray", ray_h, ray_v), ("w1", w1_h, w1_v),
        ("w2", w2_h, w2_v), ("wd", wd_h, wd_v), ("cnt", cnt_h, cnt_v), ("stp", stp_h, stp_v),
        ("wf", wf_h, wf_v),
        ("tgt", tgt_h.at[pl.ds(pl.multiple_of(core * HALF, HALF), HALF), :], tgt_v),
    )):
        bring[name] = pltpu.make_async_copy(src, dst, loc.at[i])
        bring[name].start()

    barrier = pltpu.get_barrier_semaphore()
    each_cell(lambda t: pl.semaphore_signal(barrier, inc=1, device_id=cell_device(t), device_id_type=MESH))
    pl.semaphore_signal(barrier, inc=1, device_id=sibling, device_id_type=MESH)
    each_group(lambda t: pl.semaphore_signal(barrier, inc=1, device_id=rays_device(t), device_id_type=MESH))

    for name in ("ent", "pos", "ray", "w1"):
        bring[name].wait()
    post[...] = pos_v[...].astype(F32).T.astype(BF16)
    rayt[...] = ray_v[...].astype(F32).T
    w1t[...] = w1_v[...].astype(F32).T.astype(BF16)
    for name in ("w2", "wd", "cnt", "stp"):
        bring[name].wait()
    w2t[...] = w2_v[...].T.astype(BF16)
    width = wd_v.shape[1]
    n_rows = ray_v.shape[0]
    wdb[...] = jnp.broadcast_to(wd_v[...].astype(F32), (n_rows, width)).T
    slot = lax.broadcasted_iota(jnp.int32, (pos_v.shape[0], n_rows), 0)

    def forward(k):
        hot = jnp.where(slot == ent_v[...] + k, 1.0, 0.0).astype(BF16)
        inputs = (mm(post[...], hot) + rayt[...]).astype(BF16)
        first = jnp.maximum(mm(w1t[...], inputs), 0.0).astype(BF16)
        second = jnp.maximum(mm(w2t[...], first), 0.0).astype(BF16)
        h1[k] = first
        h2[k] = second
        lg[pl.ds(k, 1), :] = jnp.sum(second.astype(F32) * wdb[...], axis=0, keepdims=True)

    def two(i, n):
        forward(2 * i)
        forward(2 * i + 1)
        return n

    lax.fori_loop(0, SAMPLES // 2, two, 0)

    order = lax.broadcasted_iota(jnp.int32, (SAMPLES, n_rows), 0)
    logit = lg[...]
    travel = jnp.where(order < cnt_v[...], stp_v[...], 0.0)
    step_depth = (jnp.maximum(logit, 0.0) + jnp.log1p(jnp.exp(-jnp.abs(logit)))) * travel

    def ahead_of(v):
        total = v
        for shift in (1, 2, 4):
            total = total + jnp.where(order >= shift, pltpu.roll(total, shift, 0), 0.0)
        return total - v

    ahead = jnp.exp(-ahead_of(step_depth))
    kept = jnp.exp(-step_depth)
    weight = ahead * (1.0 - kept)
    depth = jnp.sum(step_depth, axis=0, keepdims=True)

    def put_rows(buf, at, row):
        for half in range(2):
            buf[at, pl.ds(half, 1), :] = row[:, half * HALF:(half + 1) * HALF]

    put_rows(dep, cell, depth)
    pl.semaphore_wait(barrier, n_cell - 1 + n_rays - 1)

    def to_cells(buf, i):
        each_cell(lambda t: pltpu.make_async_remote_copy(
            buf.at[cell], buf.at[cell], many_send.at[i], many_recv.at[i],
            device_id=cell_device(t), device_id_type=MESH).start())

    def to_groups(src, dst, i):
        each_group(lambda t: pltpu.make_async_remote_copy(
            src(t), dst.at[group], many_send.at[i], many_recv.at[i],
            device_id=rays_device(t), device_id_type=MESH).start())

    def wait_many(buf, sem, i, left_out):
        part = buf.at[pl.ds(0, buf.shape[0] - left_out)]
        pltpu.make_async_copy(part, part, sem.at[i]).wait()

    sent, blocks = [], []

    def send(src, dst, i, device):
        copy = pltpu.make_async_remote_copy(
            src, dst, one_send.at[i], one_recv.at[i], device_id=device, device_id_type=MESH)
        copy.start()
        sent.append(copy)

    def arrived(dst, i):
        pltpu.make_async_copy(dst, dst, one_recv.at[i]).wait()

    def send_block(src, dst, i, at, device):
        copy = pltpu.make_async_remote_copy(
            src, dst, blk_send.at[len(blocks)], blk_recv.at[i, at], device_id=device, device_id_type=MESH)
        copy.start()
        sent.append(copy)
        blocks.append(copy)

    def block_arrived(dst, i, at):
        pltpu.make_async_copy(dst, dst, blk_recv.at[i, at]).wait()

    send(dep.at[cell], dep.at[cell], 5, sibling)
    to_cells(dep, 0)

    gather = weight[0:1] * h2[0].astype(F32)
    for k in range(1, SAMPLES):
        gather = gather + weight[k:k + 1] * h2[k].astype(F32)
    gathered = gather.astype(BF16)
    bring["wf"].wait()
    wfb[...] = wf_v[...].astype(BF16)
    wft[...] = wf_v[...].T.astype(BF16)
    partial = mm(wft[...], gathered).astype(BF16)
    for half in range(2):
        pl_s[half] = partial[:, half * HALF:(half + 1) * HALF].reshape(pl_s.shape[1:])
    send(pl_s.at[other], pr_s, 0, sibling)

    arrived(dep.at[2 * z + other], 5)
    nearer = jnp.exp(-dep[2 * z, pl.ds(core, 1), :])
    mine = jnp.where(core == 0, 1.0, nearer)
    theirs = jnp.where(core == 0, nearer, 1.0)
    arrived(pr_s, 0)
    for i in range(16):
        ns_s[i // 4, i % 4] = (mine * pl_s[core, i].astype(F32) + theirs * pr_s[i].astype(F32)).astype(BF16)

    def turn(a):
        return lax.rem(res + a + 4, 4)

    across = turn(2)
    send(ns_s.at[:, turn(3)], nr_s.at[0], 1, chip_device(z + 1))
    send(ns_s.at[:, turn(1)], nr_s.at[1], 2, chip_device(z - 1))
    send(ns_s.at[pl.ds(0, 2), res], nr_s.at[2, pl.ds(0, 2)], 3, chip_device(z + 2))
    send(ns_s.at[pl.ds(2, 2), res], nr_s.at[2, pl.ds(2, 2)], 4, chip_device(z - 2))
    bring["tgt"].wait()
    tgt_t[...] = tgt_v[...].astype(F32).T.reshape(tgt_t.shape)

    wait_many(dep, many_recv, 0, 2)
    number = lax.broadcasted_iota(jnp.int32, dep.shape, 0)
    depths = dep[...]

    def light(end):
        return jnp.exp(-jnp.sum(jnp.where(number < end, depths, 0.0), axis=0))

    for i, a in enumerate((0, -1, 1, -2, 2)):
        tt[i] = light(2 * lax.rem(z + a + n_z, n_z))
    tt[5] = light(cell)
    lights = [tt[i, pl.ds(core, 1), :] for i in range(5)]
    arrived(nr_s.at[0], 1)
    arrived(nr_s.at[1], 2)
    arrived(nr_s.at[2, pl.ds(0, 2)], 3)
    arrived(nr_s.at[2, pl.ds(2, 2)], 4)
    for i in range(4):
        fs_s[i] = (
            lights[0] * ns_s[i, across].astype(F32) + lights[1] * nr_s[0, i].astype(F32)
            + lights[2] * nr_s[1, i].astype(F32) + lights[3 + i // 2] * nr_s[2, i].astype(F32)
        ).astype(BF16)
    for a in (6, -6, 2, -2):
        to = lax.rem(z + a + n_z, n_z)
        send_block(fs_s.at[lax.div(to, 4)], fr_s.at[quad], 0, quad, chip_device(to))
    for i in range(4):
        block_arrived(fr_s.at[i], 0, i)
    lit = fr_s[0].astype(F32) + fr_s[1].astype(F32) + fr_s[2].astype(F32) + fr_s[3].astype(F32)

    own_s[...] = (lit - tgt_t[z]).astype(BF16)
    for a in (6, -6, 2, -2):
        send_block(own_s, rs_s.at[core, quad, res], 1, quad, chip_device(z + a + n_z))
    cp_s[...] = lit.reshape(cp_s.shape)
    send(cp_s.at[other], cr_s, 6, sibling)
    for a in (2, -2, 6, -6):
        at = lax.div(lax.rem(z + a + n_z, n_z), 4)
        block = rs_s.at[core, at, across]
        block_arrived(block, 1, at)
        send_block(block, block, 2, at, chip_device(z + 1))
        send_block(block, block, 3, at, chip_device(z - 1))
        send_block(block, block, 4, at, chip_device(z + 2 + 12 * lax.div(at, 2)))
        send_block(block, block, 5, at, sibling)
    for a in (2, -2, 6, -6):
        for i, beside, which in ((2, -1, turn(1)), (3, 1, turn(3)), (4, 2, res)):
            at = lax.div(lax.rem(z + beside + a + n_z, n_z), 4)
            block = rs_s.at[core, at, which]
            block_arrived(block, i, at)
            send_block(block, block, 4 + i, at, sibling)
    for i, which in ((5, across), (6, turn(1)), (7, turn(3)), (8, res)):
        for at in range(4):
            block_arrived(rs_s.at[other, at, which], i, at)

    transmit = tt[5]
    for half in range(2):
        block = rs_s[half].reshape(gp.shape[0], HALF).astype(F32)
        gp[:, half * HALF:(half + 1) * HALF] = (block * transmit[half:half + 1]).astype(BF16)
    q_t[...] = mm(wfb[...], gp[...])
    slopes = []
    for k in range(SAMPLES):
        slopes.append(jnp.sum(h2[k].astype(F32) * q_t[...], axis=0, keepdims=True))
    slope = jnp.concatenate(slopes, axis=0)
    lit_slope = weight * slope
    put_rows(br, cell, jnp.sum(lit_slope, axis=0, keepdims=True))
    send(br.at[cell], br.at[cell], 7, sibling)
    to_cells(br, 1)
    gf_s[...] = nt_dot(gathered, gp[...]).astype(BF16).reshape(gf_s.shape)
    to_groups(lambda t: gf_s.at[t], gf_r, 2)

    arrived(cr_s, 6)
    first_half = jnp.where(core == 0, cp_s[core], cr_s[...])
    second_half = jnp.where(core == 0, cr_s[...], cp_s[core])
    ren_o[...] = jnp.concatenate([first_half, second_half], axis=1).astype(BF16)
    gf_r[group] = gf_s[group]
    after = jnp.sum(lit_slope, axis=0, keepdims=True) - ahead_of(lit_slope) - lit_slope
    slope_step = slope * (ahead * kept) - after
    slope_scale = travel / (1.0 + jnp.exp(-logit))

    arrived(br.at[2 * z + other], 7)
    wait_many(br, many_recv, 1, 2)
    later = jnp.sum(jnp.where(number > cell, br[...], 0.0), axis=0)
    grad_depth = -jnp.concatenate([later[0:1], later[1:2]], axis=1)
    dg_o[...] = grad_depth
    grad_logit = (grad_depth + slope_step) * slope_scale
    grad_second = None
    for k in range(SAMPLES):
        grad = weight[k:k + 1] * q_t[...] + grad_logit[k:k + 1] * wdb[...]
        grad = jnp.where(h2[k].astype(F32) > 0.0, grad, 0.0).astype(BF16)
        term = nt_dot(h1[k], grad)
        grad_second = term if k == 0 else grad_second + term
    gs_s[...] = grad_second.astype(BF16).reshape(gs_s.shape)
    to_groups(lambda t: gs_s.at[t], gs_r, 3)
    gs_r[group] = gs_s[group]

    def folded(share):
        squares = jnp.sum(share * share, axis=0, keepdims=True)
        return sum(squares[:, i:i + HALF] for i in range(0, squares.shape[1], HALF))

    wait_many(gf_r, many_recv, 2, 1)
    share_feature = jnp.sum(gf_r[...].astype(F32), axis=0)
    square_feature = folded(share_feature)
    fa_s[...] = share_feature.astype(BF16)
    to_groups(lambda t: fa_s, gf_o, 5)
    own_feature = pltpu.make_async_copy(fa_s, gf_o.at[group], loc.at[10])
    own_feature.start()
    wait_many(gs_r, many_recv, 3, 1)
    share_second = jnp.sum(gs_r[...].astype(F32), axis=0)
    sq[cell] = square_feature + folded(share_second)
    send(sq.at[cell], sq.at[cell], 8, sibling)
    to_cells(sq, 4)
    sa_s[...] = share_second.astype(BF16)
    to_groups(lambda t: sa_s, gs_o, 6)
    own_second = pltpu.make_async_copy(sa_s, gs_o.at[group], loc.at[11])
    own_second.start()
    arrived(sq.at[2 * z + other], 8)
    wait_many(sq, many_recv, 4, 2)
    sr[group] = jnp.sum(sq[...], axis=0)
    to_groups(lambda t: sr.at[group], sr, 7)
    wait_many(gf_o, many_recv, 5, 1)
    wait_many(gs_o, many_recv, 6, 1)
    own_feature.wait()
    own_second.wait()
    for copy in sent:
        copy.wait_send()
    for i, (buf, left_out) in enumerate((
        (dep, 2), (br, 2), (gf_r, 1), (gs_r, 1), (sq, 2), (gf_o, 1), (gs_o, 1), (sr, 1),
    )):
        wait_many(buf, many_send, i, left_out)
    wait_many(sr, many_recv, 7, 1)
    sum_o[...] = jnp.sum(sr[...], axis=0)


def adam_kernel(
    entries,
    ren_h, dg_h, gs_h, gf_h, sum_h, ms_h, vs_h, mf_h, vf_h,
    ren_o, dg_o, us_o, uf_o,
    gs_v, gf_v, sum_v, ms_v, vs_v, mf_v, vf_v, us_v, uf_v,
    sem, feed, drain,
):
    n_rays, per, _ = gs_v.shape
    parts = feed.shape[0]
    groups, rows = n_rays // parts, per * n_rays // parts
    start = []
    for i, (src, dst) in enumerate((
        (sum_h, sum_v), (gs_h, gs_v), (ms_h, ms_v), (vs_h, vs_v), (ren_h, ren_o), (dg_h, dg_o),
    )):
        copy = pltpu.make_async_copy(src, dst, sem.at[i])
        copy.start()
        start.append(copy)
    fed = []
    for i in range(parts):
        some, block = pl.ds(i * rows, rows), pl.ds(i * groups, groups)
        copies = [
            pltpu.make_async_copy(gf_h.at[block], gf_v.at[block], feed.at[i, 0]),
            pltpu.make_async_copy(mf_h.at[some], mf_v.at[some], feed.at[i, 1]),
            pltpu.make_async_copy(vf_h.at[some], vf_v.at[some], feed.at[i, 2]),
        ]
        for copy in copies:
            copy.start()
        fed.append(copies)
    for copy in start[:4]:
        copy.wait()
    square_sum = jnp.sum(sum_v[...], axis=1, keepdims=True)
    rescale = lax.rsqrt(square_sum / entries + mean_floor)

    def adam(gradient, mean_moment, square_moment):
        unit = gradient.astype(F32) * rescale
        mean_new = beta_first * mean_moment + (1.0 - beta_first) * unit
        square_new = beta_second * square_moment + (1.0 - beta_second) * unit * unit
        return (mean_new / bias_first / (jnp.sqrt(square_new / bias_second) + adam_floor)).astype(BF16)

    def second(i, n):
        at = pl.ds(pl.multiple_of(i * per, per), per)
        us_v[at, :] = adam(gs_v[i], ms_v[at, :], vs_v[at, :])
        return n

    def feature(i, n):
        at = pl.ds(pl.multiple_of(i * per, per), per)
        uf_v[at, :] = adam(gf_v[i], mf_v[at, :], vf_v[at, :])
        return n

    lax.fori_loop(0, n_rays, second, 0)
    out = [pltpu.make_async_copy(us_v, us_o, sem.at[6])]
    out[0].start()
    for i in range(parts):
        for copy in fed[i]:
            copy.wait()
        lax.fori_loop(i * groups, (i + 1) * groups, feature, 0)
        some = pl.ds(i * rows, rows)
        out.append(pltpu.make_async_copy(uf_v.at[some], uf_o.at[some], drain.at[i]))
        out[-1].start()
    for copy in out + start[4:]:
        copy.wait()


def on_device(sizes, ray_code, entry_index, sample_count, step_length, positions, w_first, w_second,
              w_density, w_feature, mean_second, square_second, mean_feature, square_feature, target_color):
    n_z, n_y, n_x, all_cells = sizes
    n_cell, n_rays = 2 * n_z, n_y * n_x
    rows, width = ray_code.shape[0], ray_code.shape[2]
    table, channels = positions.shape[1], target_color.shape[1]
    part = channels // 16
    per = width // n_rays
    vmem = pltpu.VMEM
    args = (
        ray_code.reshape(rows, width), entry_index.reshape(1, rows), sample_count.reshape(1, rows),
        step_length.reshape(1, rows), positions[0], w_first[0], w_second[0], w_density,
        w_feature[0], target_color,
    )
    moments = (mean_second[0], square_second[0], mean_feature[0], square_feature[0])
    local = [vmem(a.shape, a.dtype) for a in args[:-1]] + [vmem((HALF, channels), BF16)]
    scratch = local + [
        vmem((width, rows), F32), vmem((width, table), BF16), vmem((width, width), BF16),
        vmem((width, width), BF16), vmem((channels, width), BF16), vmem((width, channels), BF16),
        vmem((width, rows), F32), vmem((SAMPLES, width, rows), BF16), vmem((SAMPLES, width, rows), BF16),
        vmem((SAMPLES, rows), F32), vmem((16, part, HALF), F32), vmem((width, rows), F32),
        vmem((channels, rows), BF16),
        vmem((n_cell, 2, HALF), F32), vmem((6, 2, HALF), F32), vmem((2, 16, part, HALF), BF16),
        vmem((16, part, HALF), BF16), vmem((4, 4, part, HALF), BF16), vmem((3, 4, part, HALF), BF16),
        vmem((4, part, HALF), BF16), vmem((4, part, HALF), BF16), vmem((2, part // 2, HALF), F32),
        vmem((part // 2, HALF), F32), vmem((part, HALF), BF16), vmem((2, 4, 4, part, HALF), BF16), vmem((n_cell, 2, HALF), F32),
        vmem((n_rays, per, channels), BF16), vmem((n_rays, per, channels), BF16),
        vmem((n_rays, per, width), BF16), vmem((n_rays, per, width), BF16),
        vmem((per, channels), BF16), vmem((per, width), BF16), vmem((n_cell, 1, HALF), F32), vmem((n_rays, 1, HALF), F32),
        pltpu.SemaphoreType.DMA((12,)), pltpu.SemaphoreType.DMA((8,)), pltpu.SemaphoreType.DMA((8,)),
        pltpu.SemaphoreType.DMA((9,)), pltpu.SemaphoreType.DMA((9,)),
        pltpu.SemaphoreType.DMA((36,)), pltpu.SemaphoreType.DMA((9, 4)),
    ]
    anywhere = pl.BlockSpec(memory_space=pl.ANY)
    inside = pl.BlockSpec(memory_space=vmem)
    found = pl.pallas_call(
        functools.partial(kernel, sizes),
        out_shape=(
            jax.ShapeDtypeStruct((part // 2, rows), BF16),
            jax.ShapeDtypeStruct((1, rows), F32),
            jax.ShapeDtypeStruct((n_rays, per, width), BF16),
            jax.ShapeDtypeStruct((n_rays, per, channels), BF16),
            jax.ShapeDtypeStruct((1, HALF), F32),
        ),
        in_specs=[anywhere] * len(args),
        out_specs=[inside, inside, anywhere, anywhere, inside],
        scratch_shapes=scratch,
        compiler_params=pltpu.CompilerParams(
            collective_id=0, has_side_effects=True, vmem_limit_bytes=62 * 1024 * 1024
        ),
    )(*args)
    parts = 4
    rendered, depth_grad, update_second, update_feature = pl.pallas_call(
        functools.partial(adam_kernel, all_cells * width * (width + channels)),
        out_shape=(
            jax.ShapeDtypeStruct((part // 2, rows), BF16),
            jax.ShapeDtypeStruct((1, rows), F32),
            jax.ShapeDtypeStruct((width, width), BF16),
            jax.ShapeDtypeStruct((width, channels), BF16),
        ),
        in_specs=[anywhere] * 9,
        out_specs=[anywhere] * 4,
        scratch_shapes=[
            vmem((n_rays, per, width), BF16), vmem((n_rays, per, channels), BF16), vmem((1, HALF), F32),
            *(vmem(m.shape, F32) for m in moments),
            vmem((width, width), BF16), vmem((width, channels), BF16),
            pltpu.SemaphoreType.DMA((7,)), pltpu.SemaphoreType.DMA((parts, 3)), pltpu.SemaphoreType.DMA((parts,)),
        ],
        compiler_params=pltpu.CompilerParams(vmem_limit_bytes=62 * 1024 * 1024),
    )(*found, *moments)
    return (rendered.T, depth_grad.reshape(rows, 1), update_second[None], update_feature[None])


def solution(mesh):
    n_cell, n_rays = mesh.devices.shape
    n_y = 4 if n_rays == 16 else 1
    sizes = (n_cell // 2, n_y, n_rays // n_y, n_cell)
    split = Mesh(mesh.devices.reshape(n_cell // 2, 2, n_y, n_rays // n_y), ("z", "core", "y", "x"))
    return jax.shard_map(
        functools.partial(on_device, sizes),
        mesh=split,
        in_specs=(
            P(RAYS, CELL, None),
            P(RAYS, CELL),
            P(RAYS, CELL),
            P(RAYS, CELL),
            P(CELL, None, None),
            P(CELL, None, None),
            P(CELL, None, None),
            P(CELL, None),
            P(CELL, None, None),
            P(CELL, None, None),
            P(CELL, None, None),
            P(CELL, None, None),
            P(CELL, None, None),
            P(RAYS, None),
        ),
        out_specs=(P(RAYS, CELL), P(RAYS, CELL), P(CELL, None, None), P(CELL, None, None)),
        check_vma=False,
    )
```

```python
import functools

import jax
import jax.numpy as jnp
from jax import lax
from jax.experimental import pallas as pl
from jax.experimental.pallas import tpu as pltpu
from jax.sharding import Mesh
from jax.sharding import PartitionSpec as P

SAMPLES = 8
MESH = pl.DeviceIdType.MESH
CELL = ("z", "core")
RAYS = ("y", "x")
HALF = 128
F32 = jnp.float32
BF16 = jnp.bfloat16

beta_first = 0.9
beta_second = 0.999
bias_first = 0.19
bias_second = 0.001999
adam_floor = 1e-08
mean_floor = 1e-06


def nt_dot(a, b):
    return lax.dot_general(a, b, (((1,), (1,)), ((), ())), preferred_element_type=F32)


def mm(a, b):
    return jnp.dot(a, b, preferred_element_type=F32)


def kernel(
    sizes,
    ray_h, ent_h, cnt_h, stp_h, pos_h, w1_h, w2_h, wd_h, wf_h,
    tgt_h,
    ren_o, dg_o, gs_o, gf_o, sum_o,
    ray_v, ent_v, cnt_v, stp_v, pos_v, w1_v, w2_v, wd_v, wf_v,
    tgt_v,
    rayt, post, w1t, w2t, wft, wfb, wdb, h1, h2, lg, tgt_t, q_t, gp,
    dep, tt, pl_s, pr_s, ns_s, nr_s, fs_s, fr_s, cp_s, cr_s, own_s, rs_s, br, pb, rb, lp,
    gf_s, gf_r, gs_s, gs_r, fa_s, sa_s, sq, sr,
    loc, many_send, many_recv, one_send, one_recv, blk_send, blk_recv,
):
    n_z, n_y, n_x, _ = sizes
    n_cell, n_rays = 2 * n_z, n_y * n_x
    z, core = lax.axis_index("z"), lax.axis_index("core")
    y, x = lax.axis_index("y"), lax.axis_index("x")
    cell = 2 * z + core
    group = n_x * y + x
    quad, res = lax.div(z, 4), lax.rem(z, 4)
    other = 1 - core

    def cell_device(t):
        return (lax.div(t, 2), lax.rem(t, 2), y, x)

    def rays_device(t):
        return (z, core, lax.div(t, n_x), lax.rem(t, n_x))

    def chip_device(t):
        return (lax.rem(t + n_z, n_z), core, y, x)

    sibling = (z, other, y, x)

    def each_cell(send):
        def step(j, n):
            to = lax.rem(z + 1 + lax.rem(lax.div(j, 2) + n_z // 2 - 2, n_z - 1), n_z)
            send(2 * to + lax.rem(j, 2))
            return n

        lax.fori_loop(0, n_cell - 2, step, 0)

    def each_group(send):
        def step(j, n):
            to_y = lax.rem(y + lax.div(j, n_x), n_y)
            to_x = lax.rem(x + lax.rem(j, n_x), n_x)
            send(to_y * n_x + to_x)
            return n

        lax.fori_loop(1, n_rays, step, 0)

    bring = {}
    for i, (name, src, dst) in enumerate((
        ("ent", ent_h, ent_v), ("pos", pos_h, pos_v), ("ray", ray_h, ray_v), ("w1", w1_h, w1_v),
        ("w2", w2_h, w2_v), ("wd", wd_h, wd_v), ("cnt", cnt_h, cnt_v), ("stp", stp_h, stp_v),
        ("wf", wf_h, wf_v),
        ("tgt", tgt_h.at[pl.ds(pl.multiple_of(core * HALF, HALF), HALF), :], tgt_v),
    )):
        bring[name] = pltpu.make_async_copy(src, dst, loc.at[i])
        bring[name].start()

    barrier = pltpu.get_barrier_semaphore()
    each_cell(lambda t: pl.semaphore_signal(barrier, inc=1, device_id=cell_device(t), device_id_type=MESH))
    pl.semaphore_signal(barrier, inc=1, device_id=sibling, device_id_type=MESH)
    each_group(lambda t: pl.semaphore_signal(barrier, inc=1, device_id=rays_device(t), device_id_type=MESH))

    for name in ("ent", "pos", "ray", "w1"):
        bring[name].wait()
    post[...] = pos_v[...].astype(F32).T.astype(BF16)
    rayt[...] = ray_v[...].astype(F32).T
    w1t[...] = w1_v[...].astype(F32).T.astype(BF16)
    for name in ("w2", "wd", "cnt", "stp"):
        bring[name].wait()
    w2t[...] = w2_v[...].T.astype(BF16)
    width = wd_v.shape[1]
    n_rows = ray_v.shape[0]
    wdb[...] = jnp.broadcast_to(wd_v[...].astype(F32), (n_rows, width)).T
    slot = lax.broadcasted_iota(jnp.int32, (pos_v.shape[0], n_rows), 0)

    def forward(k):
        hot = jnp.where(slot == ent_v[...] + k, 1.0, 0.0).astype(BF16)
        inputs = (mm(post[...], hot) + rayt[...]).astype(BF16)
        first = jnp.maximum(mm(w1t[...], inputs), 0.0).astype(BF16)
        second = jnp.maximum(mm(w2t[...], first), 0.0).astype(BF16)
        h1[k] = first
        h2[k] = second
        lg[pl.ds(k, 1), :] = jnp.sum(second.astype(F32) * wdb[...], axis=0, keepdims=True)

    def two(i, n):
        forward(2 * i)
        forward(2 * i + 1)
        return n

    lax.fori_loop(0, SAMPLES // 2, two, 0)

    order = lax.broadcasted_iota(jnp.int32, (SAMPLES, n_rows), 0)
    logit = lg[...]
    travel = jnp.where(order < cnt_v[...], stp_v[...], 0.0)
    step_depth = (jnp.maximum(logit, 0.0) + jnp.log1p(jnp.exp(-jnp.abs(logit)))) * travel

    def ahead_of(v):
        total = v
        for shift in (1, 2, 4):
            total = total + jnp.where(order >= shift, pltpu.roll(total, shift, 0), 0.0)
        return total - v

    ahead = jnp.exp(-ahead_of(step_depth))
    kept = jnp.exp(-step_depth)
    weight = ahead * (1.0 - kept)
    depth = jnp.sum(step_depth, axis=0, keepdims=True)

    def put_rows(buf, at, row):
        for half in range(2):
            buf[at, pl.ds(half, 1), :] = row[:, half * HALF:(half + 1) * HALF]

    put_rows(dep, cell, depth)
    pl.semaphore_wait(barrier, n_cell - 1 + n_rays - 1)

    def to_cells(buf, i):
        each_cell(lambda t: pltpu.make_async_remote_copy(
            buf.at[cell], buf.at[cell], many_send.at[i], many_recv.at[i],
            device_id=cell_device(t), device_id_type=MESH).start())

    def to_groups(src, dst, i):
        each_group(lambda t: pltpu.make_async_remote_copy(
            src(t), dst.at[group], many_send.at[i], many_recv.at[i],
            device_id=rays_device(t), device_id_type=MESH).start())

    def wait_many(buf, sem, i, left_out):
        part = buf.at[pl.ds(0, buf.shape[0] - left_out)]
        pltpu.make_async_copy(part, part, sem.at[i]).wait()

    sent, blocks = [], []

    def send(src, dst, i, device):
        copy = pltpu.make_async_remote_copy(
            src, dst, one_send.at[i], one_recv.at[i], device_id=device, device_id_type=MESH)
        copy.start()
        sent.append(copy)

    def arrived(dst, i):
        pltpu.make_async_copy(dst, dst, one_recv.at[i]).wait()

    def send_block(src, dst, i, at, device):
        copy = pltpu.make_async_remote_copy(
            src, dst, blk_send.at[len(blocks)], blk_recv.at[i, at], device_id=device, device_id_type=MESH)
        copy.start()
        sent.append(copy)
        blocks.append(copy)

    def block_arrived(dst, i, at):
        pltpu.make_async_copy(dst, dst, blk_recv.at[i, at]).wait()

    send(dep.at[cell], dep.at[cell], 5, sibling)
    to_cells(dep, 0)

    gather = weight[0:1] * h2[0].astype(F32)
    for k in range(1, SAMPLES):
        gather = gather + weight[k:k + 1] * h2[k].astype(F32)
    gathered = gather.astype(BF16)
    bring["wf"].wait()
    wfb[...] = wf_v[...].astype(BF16)
    wft[...] = wf_v[...].T.astype(BF16)
    partial = mm(wft[...], gathered).astype(BF16)
    for half in range(2):
        pl_s[half] = partial[:, half * HALF:(half + 1) * HALF].reshape(pl_s.shape[1:])
    send(pl_s.at[other], pr_s, 0, sibling)

    arrived(dep.at[2 * z + other], 5)
    nearer = jnp.exp(-dep[2 * z, pl.ds(core, 1), :])
    mine = jnp.where(core == 0, 1.0, nearer)
    theirs = jnp.where(core == 0, nearer, 1.0)
    arrived(pr_s, 0)
    for i in range(16):
        ns_s[i // 4, i % 4] = (mine * pl_s[core, i].astype(F32) + theirs * pr_s[i].astype(F32)).astype(BF16)

    def turn(a):
        return lax.rem(res + a + 4, 4)

    across = turn(2)
    send(ns_s.at[:, turn(3)], nr_s.at[0], 1, chip_device(z + 1))
    send(ns_s.at[:, turn(1)], nr_s.at[1], 2, chip_device(z - 1))
    send(ns_s.at[pl.ds(0, 2), res], nr_s.at[2, pl.ds(0, 2)], 3, chip_device(z + 2))
    send(ns_s.at[pl.ds(2, 2), res], nr_s.at[2, pl.ds(2, 2)], 4, chip_device(z - 2))
    bring["tgt"].wait()
    tgt_t[...] = tgt_v[...].astype(F32).T.reshape(tgt_t.shape)

    wait_many(dep, many_recv, 0, 2)
    number = lax.broadcasted_iota(jnp.int32, dep.shape, 0)
    depths = dep[...]

    def light(end):
        return jnp.exp(-jnp.sum(jnp.where(number < end, depths, 0.0), axis=0))

    for i, a in enumerate((0, -1, 1, -2, 2)):
        tt[i] = light(2 * lax.rem(z + a + n_z, n_z))
    tt[5] = light(cell)
    lights = [tt[i, pl.ds(core, 1), :] for i in range(5)]
    arrived(nr_s.at[0], 1)
    arrived(nr_s.at[1], 2)
    arrived(nr_s.at[2, pl.ds(0, 2)], 3)
    arrived(nr_s.at[2, pl.ds(2, 2)], 4)
    for i in range(4):
        fs_s[i] = (
            lights[0] * ns_s[i, across].astype(F32) + lights[1] * nr_s[0, i].astype(F32)
            + lights[2] * nr_s[1, i].astype(F32) + lights[3 + i // 2] * nr_s[2, i].astype(F32)
        ).astype(BF16)
    for a in (6, -6, 2, -2):
        to = lax.rem(z + a + n_z, n_z)
        send_block(fs_s.at[lax.div(to, 4)], fr_s.at[quad], 0, quad, chip_device(to))
    for i in range(4):
        block_arrived(fr_s.at[i], 0, i)
    lit = fr_s[0].astype(F32) + fr_s[1].astype(F32) + fr_s[2].astype(F32) + fr_s[3].astype(F32)

    own_s[...] = (lit - tgt_t[z]).astype(BF16)
    for a in (6, -6, 2, -2):
        send_block(own_s, rs_s.at[core, quad, res], 1, quad, chip_device(z + a + n_z))
    cp_s[...] = lit.reshape(cp_s.shape)
    send(cp_s.at[other], cr_s, 6, sibling)
    for a in (2, -2, 6, -6):
        at = lax.div(lax.rem(z + a + n_z, n_z), 4)
        block = rs_s.at[core, at, across]
        block_arrived(block, 1, at)
        send_block(block, block, 2, at, chip_device(z + 1))
        send_block(block, block, 3, at, chip_device(z - 1))
        send_block(block, block, 4, at, chip_device(z + 2 + 12 * lax.div(at, 2)))
        send_block(block, block, 5, at, sibling)
    sources = ((0, 0), (-1, 1), (1, 2), (-2, 3), (2, 4))
    lit_rows = [0.0] * 5
    for i in range(4):
        block = rs_s[core, i, across].astype(F32)
        for j, piece in ((0, ns_s[i, across]), (1, nr_s[0, i]), (2, nr_s[1, i]), (3 + i // 2, nr_s[2, i])):
            lit_rows[j] = lit_rows[j] + block * piece.astype(F32)
    chip = lax.broadcasted_iota(jnp.int32, (n_z, HALF), 0)
    behind = jnp.zeros((n_z, HALF), F32)
    for a, j in sources:
        row = lights[j] * jnp.sum(lit_rows[j], axis=0, keepdims=True)
        behind = behind + jnp.where(chip < lax.rem(z + a + n_z, n_z), row, 0.0)
    for i in range(n_z):
        pb[i] = behind[i:i + 1]

    def to_chip(j, n):
        to = lax.rem(z + 1 + lax.rem(j + n_z // 2 - 1, n_z - 1), n_z)
        pltpu.make_async_remote_copy(
            pb.at[to], rb.at[z], many_send.at[1], many_recv.at[1],
            device_id=(to, core, y, x), device_id_type=MESH).start()
        return n

    lax.fori_loop(0, n_z - 1, to_chip, 0)
    rb[z] = pb[z]

    for a in (2, -2, 6, -6):
        for i, beside, which in ((2, -1, turn(1)), (3, 1, turn(3)), (4, 2, res)):
            at = lax.div(lax.rem(z + beside + a + n_z, n_z), 4)
            block = rs_s.at[core, at, which]
            block_arrived(block, i, at)
            send_block(block, block, 4 + i, at, sibling)
    for i, which in ((5, across), (6, turn(1)), (7, turn(3)), (8, res)):
        for at in range(4):
            block_arrived(rs_s.at[other, at, which], i, at)

    transmit = tt[5]
    for half in range(2):
        block = rs_s[half].reshape(gp.shape[0], HALF).astype(F32)
        gp[:, half * HALF:(half + 1) * HALF] = (block * transmit[half:half + 1]).astype(BF16)
    q_t[...] = mm(wfb[...], gp[...])
    slopes = []
    for k in range(SAMPLES):
        slopes.append(jnp.sum(h2[k].astype(F32) * q_t[...], axis=0, keepdims=True))
    slope = jnp.concatenate(slopes, axis=0)
    lit_slope = weight * slope
    put_rows(br, core, jnp.sum(lit_slope, axis=0, keepdims=True))
    send(br.at[core], br.at[core], 7, sibling)
    gf_s[...] = nt_dot(gathered, gp[...]).astype(BF16).reshape(gf_s.shape)
    to_groups(lambda t: gf_s.at[t], gf_r, 2)

    arrived(cr_s, 6)
    first_half = jnp.where(core == 0, cp_s[core], cr_s[...])
    second_half = jnp.where(core == 0, cr_s[...], cp_s[core])
    ren_o[...] = jnp.concatenate([first_half, second_half], axis=1).astype(BF16)
    gf_r[group] = gf_s[group]
    after = jnp.sum(lit_slope, axis=0, keepdims=True) - ahead_of(lit_slope) - lit_slope
    slope_step = slope * (ahead * kept) - after
    slope_scale = travel / (1.0 + jnp.exp(-logit))

    wait_many(rb, many_recv, 1, 1)
    lp[core] = jnp.sum(rb[...], axis=0)
    send(lp.at[core], lp.at[core], 9, sibling)
    arrived(br.at[other], 7)
    follower = jnp.where(core == 0, br[1], 0.0)
    arrived(lp.at[other], 9)
    grad_depth = -jnp.concatenate([lp[0] + follower[0:1], lp[1] + follower[1:2]], axis=1)
    dg_o[...] = grad_depth
    grad_logit = (grad_depth + slope_step) * slope_scale
    grad_second = None
    for k in range(SAMPLES):
        grad = weight[k:k + 1] * q_t[...] + grad_logit[k:k + 1] * wdb[...]
        grad = jnp.where(h2[k].astype(F32) > 0.0, grad, 0.0).astype(BF16)
        term = nt_dot(h1[k], grad)
        grad_second = term if k == 0 else grad_second + term
    gs_s[...] = grad_second.astype(BF16).reshape(gs_s.shape)
    to_groups(lambda t: gs_s.at[t], gs_r, 3)
    gs_r[group] = gs_s[group]

    def folded(share):
        squares = jnp.sum(share * share, axis=0, keepdims=True)
        return sum(squares[:, i:i + HALF] for i in range(0, squares.shape[1], HALF))

    wait_many(gf_r, many_recv, 2, 1)
    share_feature = jnp.sum(gf_r[...].astype(F32), axis=0)
    square_feature = folded(share_feature)
    fa_s[...] = share_feature.astype(BF16)
    to_groups(lambda t: fa_s, gf_o, 5)
    own_feature = pltpu.make_async_copy(fa_s, gf_o.at[group], loc.at[10])
    own_feature.start()
    wait_many(gs_r, many_recv, 3, 1)
    share_second = jnp.sum(gs_r[...].astype(F32), axis=0)
    sq[cell] = square_feature + folded(share_second)
    send(sq.at[cell], sq.at[cell], 8, sibling)
    to_cells(sq, 4)
    sa_s[...] = share_second.astype(BF16)
    to_groups(lambda t: sa_s, gs_o, 6)
    own_second = pltpu.make_async_copy(sa_s, gs_o.at[group], loc.at[11])
    own_second.start()
    arrived(sq.at[2 * z + other], 8)
    wait_many(sq, many_recv, 4, 2)
    sr[group] = jnp.sum(sq[...], axis=0)
    to_groups(lambda t: sr.at[group], sr, 7)
    wait_many(gf_o, many_recv, 5, 1)
    wait_many(gs_o, many_recv, 6, 1)
    own_feature.wait()
    own_second.wait()
    for copy in sent:
        copy.wait_send()
    for i, (buf, left_out) in enumerate((
        (dep, 2), (rb, 1), (gf_r, 1), (gs_r, 1), (sq, 2), (gf_o, 1), (gs_o, 1), (sr, 1),
    )):
        wait_many(buf, many_send, i, left_out)
    wait_many(sr, many_recv, 7, 1)
    sum_o[...] = jnp.sum(sr[...], axis=0)


def adam_kernel(
    entries,
    ren_h, dg_h, gs_h, gf_h, sum_h, ms_h, vs_h, mf_h, vf_h,
    ren_o, dg_o, us_o, uf_o,
    gs_v, gf_v, sum_v, ms_v, vs_v, mf_v, vf_v, us_v, uf_v,
    sem, feed, drain,
):
    n_rays, per, _ = gs_v.shape
    parts = feed.shape[0]
    groups, rows = n_rays // parts, per * n_rays // parts
    start = []
    for i, (src, dst) in enumerate((
        (sum_h, sum_v), (gs_h, gs_v), (ms_h, ms_v), (vs_h, vs_v), (ren_h, ren_o), (dg_h, dg_o),
    )):
        copy = pltpu.make_async_copy(src, dst, sem.at[i])
        copy.start()
        start.append(copy)
    fed = []
    for i in range(parts):
        some, block = pl.ds(i * rows, rows), pl.ds(i * groups, groups)
        copies = [
            pltpu.make_async_copy(gf_h.at[block], gf_v.at[block], feed.at[i, 0]),
            pltpu.make_async_copy(mf_h.at[some], mf_v.at[some], feed.at[i, 1]),
            pltpu.make_async_copy(vf_h.at[some], vf_v.at[some], feed.at[i, 2]),
        ]
        for copy in copies:
            copy.start()
        fed.append(copies)
    for copy in start[:4]:
        copy.wait()
    square_sum = jnp.sum(sum_v[...], axis=1, keepdims=True)
    rescale = lax.rsqrt(square_sum / entries + mean_floor)

    def adam(gradient, mean_moment, square_moment):
        unit = gradient.astype(F32) * rescale
        mean_new = beta_first * mean_moment + (1.0 - beta_first) * unit
        square_new = beta_second * square_moment + (1.0 - beta_second) * unit * unit
        return (mean_new / bias_first / (jnp.sqrt(square_new / bias_second) + adam_floor)).astype(BF16)

    def second(i, n):
        at = pl.ds(pl.multiple_of(i * per, per), per)
        us_v[at, :] = adam(gs_v[i], ms_v[at, :], vs_v[at, :])
        return n

    def feature(i, n):
        at = pl.ds(pl.multiple_of(i * per, per), per)
        uf_v[at, :] = adam(gf_v[i], mf_v[at, :], vf_v[at, :])
        return n

    lax.fori_loop(0, n_rays, second, 0)
    out = [pltpu.make_async_copy(us_v, us_o, sem.at[6])]
    out[0].start()
    for i in range(parts):
        for copy in fed[i]:
            copy.wait()
        lax.fori_loop(i * groups, (i + 1) * groups, feature, 0)
        some = pl.ds(i * rows, rows)
        out.append(pltpu.make_async_copy(uf_v.at[some], uf_o.at[some], drain.at[i]))
        out[-1].start()
    for copy in out + start[4:]:
        copy.wait()


def on_device(sizes, ray_code, entry_index, sample_count, step_length, positions, w_first, w_second,
              w_density, w_feature, mean_second, square_second, mean_feature, square_feature, target_color):
    n_z, n_y, n_x, all_cells = sizes
    n_cell, n_rays = 2 * n_z, n_y * n_x
    rows, width = ray_code.shape[0], ray_code.shape[2]
    table, channels = positions.shape[1], target_color.shape[1]
    part = channels // 16
    per = width // n_rays
    vmem = pltpu.VMEM
    args = (
        ray_code.reshape(rows, width), entry_index.reshape(1, rows), sample_count.reshape(1, rows),
        step_length.reshape(1, rows), positions[0], w_first[0], w_second[0], w_density,
        w_feature[0], target_color,
    )
    moments = (mean_second[0], square_second[0], mean_feature[0], square_feature[0])
    local = [vmem(a.shape, a.dtype) for a in args[:-1]] + [vmem((HALF, channels), BF16)]
    scratch = local + [
        vmem((width, rows), F32), vmem((width, table), BF16), vmem((width, width), BF16),
        vmem((width, width), BF16), vmem((channels, width), BF16), vmem((width, channels), BF16),
        vmem((width, rows), F32), vmem((SAMPLES, width, rows), BF16), vmem((SAMPLES, width, rows), BF16),
        vmem((SAMPLES, rows), F32), vmem((16, part, HALF), F32), vmem((width, rows), F32),
        vmem((channels, rows), BF16),
        vmem((n_cell, 2, HALF), F32), vmem((6, 2, HALF), F32), vmem((2, 16, part, HALF), BF16),
        vmem((16, part, HALF), BF16), vmem((4, 4, part, HALF), BF16), vmem((3, 4, part, HALF), BF16),
        vmem((4, part, HALF), BF16), vmem((4, part, HALF), BF16), vmem((2, part // 2, HALF), F32),
        vmem((part // 2, HALF), F32), vmem((part, HALF), BF16), vmem((2, 4, 4, part, HALF), BF16), vmem((2, 2, HALF), F32),
        vmem((n_z, 1, HALF), F32), vmem((n_z, 1, HALF), F32), vmem((2, 1, HALF), F32),
        vmem((n_rays, per, channels), BF16), vmem((n_rays, per, channels), BF16),
        vmem((n_rays, per, width), BF16), vmem((n_rays, per, width), BF16),
        vmem((per, channels), BF16), vmem((per, width), BF16), vmem((n_cell, 1, HALF), F32), vmem((n_rays, 1, HALF), F32),
        pltpu.SemaphoreType.DMA((12,)), pltpu.SemaphoreType.DMA((8,)), pltpu.SemaphoreType.DMA((8,)),
        pltpu.SemaphoreType.DMA((10,)), pltpu.SemaphoreType.DMA((10,)),
        pltpu.SemaphoreType.DMA((36,)), pltpu.SemaphoreType.DMA((9, 4)),
    ]
    anywhere = pl.BlockSpec(memory_space=pl.ANY)
    inside = pl.BlockSpec(memory_space=vmem)
    found = pl.pallas_call(
        functools.partial(kernel, sizes),
        out_shape=(
            jax.ShapeDtypeStruct((part // 2, rows), BF16),
            jax.ShapeDtypeStruct((1, rows), F32),
            jax.ShapeDtypeStruct((n_rays, per, width), BF16),
            jax.ShapeDtypeStruct((n_rays, per, channels), BF16),
            jax.ShapeDtypeStruct((1, HALF), F32),
        ),
        in_specs=[anywhere] * len(args),
        out_specs=[inside, inside, anywhere, anywhere, inside],
        scratch_shapes=scratch,
        compiler_params=pltpu.CompilerParams(
            collective_id=0, has_side_effects=True, vmem_limit_bytes=62 * 1024 * 1024
        ),
    )(*args)
    parts = min(4, n_rays)
    rendered, depth_grad, update_second, update_feature = pl.pallas_call(
        functools.partial(adam_kernel, all_cells * width * (width + channels)),
        out_shape=(
            jax.ShapeDtypeStruct((part // 2, rows), BF16),
            jax.ShapeDtypeStruct((1, rows), F32),
            jax.ShapeDtypeStruct((width, width), BF16),
            jax.ShapeDtypeStruct((width, channels), BF16),
        ),
        in_specs=[anywhere] * 9,
        out_specs=[anywhere] * 4,
        scratch_shapes=[
            vmem((n_rays, per, width), BF16), vmem((n_rays, per, channels), BF16), vmem((1, HALF), F32),
            *(vmem(m.shape, F32) for m in moments),
            vmem((width, width), BF16), vmem((width, channels), BF16),
            pltpu.SemaphoreType.DMA((7,)), pltpu.SemaphoreType.DMA((parts, 3)), pltpu.SemaphoreType.DMA((parts,)),
        ],
        compiler_params=pltpu.CompilerParams(vmem_limit_bytes=62 * 1024 * 1024),
    )(*found, *moments)
    return (rendered.T, depth_grad.reshape(rows, 1), update_second[None], update_feature[None])


def solution(mesh):
    n_cell, n_rays = mesh.devices.shape
    n_y = 4 if n_rays == 16 else 1
    sizes = (n_cell // 2, n_y, n_rays // n_y, n_cell)
    split = Mesh(mesh.devices.reshape(n_cell // 2, 2, n_y, n_rays // n_y), ("z", "core", "y", "x"))
    return jax.shard_map(
        functools.partial(on_device, sizes),
        mesh=split,
        in_specs=(
            P(RAYS, CELL, None),
            P(RAYS, CELL),
            P(RAYS, CELL),
            P(RAYS, CELL),
            P(CELL, None, None),
            P(CELL, None, None),
            P(CELL, None, None),
            P(CELL, None),
            P(CELL, None, None),
            P(CELL, None, None),
            P(CELL, None, None),
            P(CELL, None, None),
            P(CELL, None, None),
            P(RAYS, None),
        ),
        out_specs=(P(RAYS, CELL), P(RAYS, CELL), P(CELL, None, None), P(CELL, None, None)),
        check_vma=False,
    )
```

```python
import functools

import jax
import jax.numpy as jnp
from jax import lax
from jax.experimental import pallas as pl
from jax.experimental.pallas import tpu as pltpu
from jax.sharding import Mesh
from jax.sharding import PartitionSpec as P

SAMPLES = 8
MESH = pl.DeviceIdType.MESH
CELL = ("z", "core")
RAYS = ("y", "x")
HALF = 128
F32 = jnp.float32
BF16 = jnp.bfloat16

beta_first = 0.9
beta_second = 0.999
bias_first = 0.19
bias_second = 0.001999
adam_floor = 1e-08
mean_floor = 1e-06


def nt_dot(a, b):
    return lax.dot_general(a, b, (((1,), (1,)), ((), ())), preferred_element_type=F32)


def mm(a, b):
    return jnp.dot(a, b, preferred_element_type=F32)


def kernel(
    sizes,
    ray_h, ent_h, cnt_h, stp_h, pos_h, w1_h, w2_h, wd_h, wf_h,
    tgt_h,
    ren_o, dg_o, gs_o, gf_o, sum_o,
    ray_v, ent_v, cnt_v, stp_v, pos_v, w1_v, w2_v, wd_v, wf_v,
    tgt_v,
    rayt, post, w2t, wft, wfb, wdb, h1, h2, lg, tgt_t, q_t, gp, gb,
    dep, tt, pl_s, pr_s, ns_s, nr_s, fs_s, fr_s, cp_s, cr_s, own_s, rs_s, br, pb, rb, lp,
    gf_s, gf_r, gs_s, gs_r, fa_s, sa_s, sq, sr,
    loc, many_send, many_recv, one_send, one_recv, blk_send, blk_recv,
):
    n_z, n_y, n_x, _ = sizes
    n_cell, n_rays = 2 * n_z, n_y * n_x
    z, core = lax.axis_index("z"), lax.axis_index("core")
    y, x = lax.axis_index("y"), lax.axis_index("x")
    cell = 2 * z + core
    group = n_x * y + x
    quad, res = lax.div(z, 4), lax.rem(z, 4)
    other = 1 - core

    def cell_device(t):
        return (lax.div(t, 2), lax.rem(t, 2), y, x)

    def rays_device(t):
        return (z, core, lax.div(t, n_x), lax.rem(t, n_x))

    def chip_device(t):
        return (lax.rem(t + n_z, n_z), core, y, x)

    sibling = (z, other, y, x)

    def away(i, n):
        half = lax.div(i + 1, 2)
        return n // 2 + half - 2 * half * lax.rem(i, 2)

    def each_cell(send):
        def step(j, n):
            send(2 * lax.rem(z + away(lax.div(j, 2), n_z), n_z) + lax.rem(j, 2))
            return n

        lax.fori_loop(0, n_cell - 2, step, 0)

    def each_group(send):
        def step(j, n):
            to_y = lax.rem(y + away(lax.div(j, n_x), n_y), n_y)
            to_x = lax.rem(x + away(lax.rem(j, n_x), n_x), n_x)
            send(to_y * n_x + to_x)
            return n

        lax.fori_loop(0, n_rays - 1, step, 0)

    bring = {}
    for i, (name, src, dst) in enumerate((
        ("ent", ent_h, ent_v), ("pos", pos_h, pos_v), ("ray", ray_h, ray_v), ("w1", w1_h, w1_v),
        ("w2", w2_h, w2_v), ("wd", wd_h, wd_v), ("cnt", cnt_h, cnt_v), ("stp", stp_h, stp_v),
        ("wf", wf_h, wf_v),
        ("tgt", tgt_h.at[pl.ds(pl.multiple_of(core * HALF, HALF), HALF), :], tgt_v),
    )):
        bring[name] = pltpu.make_async_copy(src, dst, loc.at[i])
        bring[name].start()

    barrier = pltpu.get_barrier_semaphore()
    each_cell(lambda t: pl.semaphore_signal(barrier, inc=1, device_id=cell_device(t), device_id_type=MESH))
    pl.semaphore_signal(barrier, inc=1, device_id=sibling, device_id_type=MESH)
    each_group(lambda t: pl.semaphore_signal(barrier, inc=1, device_id=rays_device(t), device_id_type=MESH))

    for name in ("pos", "ray", "w1"):
        bring[name].wait()
    width = wd_v.shape[1]
    n_rows = ray_v.shape[0]
    placed = mm(pos_v[...], w1_v[...]).T
    coarse = placed.astype(BF16)
    post[...] = jnp.concatenate([coarse, (placed - coarse.astype(F32)).astype(BF16)], axis=1)
    rayt[...] = mm(ray_v[...], w1_v[...]).T
    for name in ("w2", "wd", "ent", "cnt", "stp", "wf"):
        bring[name].wait()
    w2t[...] = w2_v[...].T.astype(BF16)
    column = jnp.broadcast_to(wd_v[...].astype(F32), (HALF, width)).T
    wdb[...] = jnp.concatenate([column] * (n_rows // HALF), axis=1)
    slot = lax.broadcasted_iota(jnp.int32, (pos_v.shape[0], n_rows), 0)
    for k in range(SAMPLES):
        hot = jnp.where(slot == ent_v[...] + k, 1.0, 0.0).astype(BF16)
        hot = jnp.concatenate([hot, hot], axis=0)
        first = jnp.maximum(mm(post[...], hot) + rayt[...], 0.0).astype(BF16)
        second = jnp.maximum(mm(w2t[...], first), 0.0).astype(BF16)
        h1[:, k * n_rows:(k + 1) * n_rows] = first
        h2[k] = second
        lg[k:k + 1] = jnp.sum(second.astype(F32) * wdb[...], axis=0, keepdims=True)

    order = lax.broadcasted_iota(jnp.int32, (SAMPLES, n_rows), 0)
    logit = lg[...]
    travel = jnp.where(order < cnt_v[...], stp_v[...], 0.0)
    step_depth = (jnp.maximum(logit, 0.0) + jnp.log1p(jnp.exp(-jnp.abs(logit)))) * travel

    def ahead_of(v):
        total = v
        for shift in (1, 2, 4):
            total = total + jnp.where(order >= shift, pltpu.roll(total, shift, 0), 0.0)
        return total - v

    ahead = jnp.exp(-ahead_of(step_depth))
    kept = jnp.exp(-step_depth)
    weight = ahead * (1.0 - kept)
    depth = jnp.sum(step_depth, axis=0, keepdims=True)

    def put_rows(buf, at, row):
        for half in range(2):
            buf[at, pl.ds(half, 1), :] = row[:, half * HALF:(half + 1) * HALF]

    put_rows(dep, cell, depth)
    pl.semaphore_wait(barrier, n_cell - 1 + n_rays - 1)

    def to_cells(buf, i):
        each_cell(lambda t: pltpu.make_async_remote_copy(
            buf.at[cell], buf.at[cell], many_send.at[i], many_recv.at[i],
            device_id=cell_device(t), device_id_type=MESH).start())

    def to_groups(src, dst, i):
        each_group(lambda t: pltpu.make_async_remote_copy(
            src(t), dst.at[group], many_send.at[i], many_recv.at[i],
            device_id=rays_device(t), device_id_type=MESH).start())

    def wait_many(buf, sem, i, left_out):
        part = buf.at[pl.ds(0, buf.shape[0] - left_out)]
        pltpu.make_async_copy(part, part, sem.at[i]).wait()

    sent, blocks = [], []

    def send(src, dst, i, device):
        copy = pltpu.make_async_remote_copy(
            src, dst, one_send.at[i], one_recv.at[i], device_id=device, device_id_type=MESH)
        copy.start()
        sent.append(copy)

    def arrived(dst, i):
        pltpu.make_async_copy(dst, dst, one_recv.at[i]).wait()

    def send_block(src, dst, i, at, device):
        copy = pltpu.make_async_remote_copy(
            src, dst, blk_send.at[len(blocks)], blk_recv.at[i, at], device_id=device, device_id_type=MESH)
        copy.start()
        sent.append(copy)
        blocks.append(copy)

    def block_arrived(dst, i, at):
        pltpu.make_async_copy(dst, dst, blk_recv.at[i, at]).wait()

    send(dep.at[cell], dep.at[cell], 5, sibling)
    to_cells(dep, 0)

    gather = weight[0:1] * h2[0].astype(F32)
    for k in range(1, SAMPLES):
        gather = gather + weight[k:k + 1] * h2[k].astype(F32)
    gathered = gather.astype(BF16)
    wfb[...] = wf_v[...].astype(BF16)
    wft[...] = wf_v[...].T.astype(BF16)
    partial = mm(wft[...], gathered).astype(BF16)
    for half in range(2):
        pl_s[half] = partial[:, half * HALF:(half + 1) * HALF].reshape(pl_s.shape[1:])
    send(pl_s.at[other], pr_s, 0, sibling)

    arrived(dep.at[2 * z + other], 5)
    nearer = jnp.exp(-dep[2 * z, pl.ds(core, 1), :])
    mine = jnp.where(core == 0, 1.0, nearer)
    theirs = jnp.where(core == 0, nearer, 1.0)
    arrived(pr_s, 0)
    for i in range(16):
        ns_s[i // 4, i % 4] = (mine * pl_s[core, i].astype(F32) + theirs * pr_s[i].astype(F32)).astype(BF16)

    def turn(a):
        return lax.rem(res + a + 4, 4)

    across = turn(2)
    send(ns_s.at[:, turn(3)], nr_s.at[0], 1, chip_device(z + 1))
    send(ns_s.at[:, turn(1)], nr_s.at[1], 2, chip_device(z - 1))
    send(ns_s.at[pl.ds(0, 2), res], nr_s.at[2, pl.ds(0, 2)], 3, chip_device(z + 2))
    send(ns_s.at[pl.ds(2, 2), res], nr_s.at[2, pl.ds(2, 2)], 4, chip_device(z - 2))
    bring["tgt"].wait()
    tgt_t[...] = tgt_v[...].astype(F32).T.reshape(tgt_t.shape)

    wait_many(dep, many_recv, 0, 2)
    number = lax.broadcasted_iota(jnp.int32, dep.shape, 0)
    depths = dep[...]

    def light(end):
        return jnp.exp(-jnp.sum(jnp.where(number < end, depths, 0.0), axis=0))

    for i, a in enumerate((0, -1, 1, -2, 2)):
        tt[i] = light(2 * lax.rem(z + a + n_z, n_z))
    tt[5] = light(cell)
    lights = [tt[i, pl.ds(core, 1), :] for i in range(5)]
    arrived(nr_s.at[0], 1)
    arrived(nr_s.at[1], 2)
    arrived(nr_s.at[2, pl.ds(0, 2)], 3)
    arrived(nr_s.at[2, pl.ds(2, 2)], 4)
    for i in range(4):
        fs_s[i] = (
            lights[0] * ns_s[i, across].astype(F32) + lights[1] * nr_s[0, i].astype(F32)
            + lights[2] * nr_s[1, i].astype(F32) + lights[3 + i // 2] * nr_s[2, i].astype(F32)
        ).astype(BF16)
    for a in (6, -6, 2, -2):
        to = lax.rem(z + a + n_z, n_z)
        send_block(fs_s.at[lax.div(to, 4)], fr_s.at[quad], 0, quad, chip_device(to))
    for i in range(4):
        block_arrived(fr_s.at[i], 0, i)
    lit = fr_s[0].astype(F32) + fr_s[1].astype(F32) + fr_s[2].astype(F32) + fr_s[3].astype(F32)

    own_s[...] = (lit - tgt_t[z]).astype(BF16)
    for a in (6, -6, 2, -2):
        send_block(own_s, rs_s.at[core, quad, res], 1, quad, chip_device(z + a + n_z))
    cp_s[...] = lit.reshape(cp_s.shape)
    send(cp_s.at[other], cr_s, 6, sibling)
    for a in (2, -2, 6, -6):
        at = lax.div(lax.rem(z + a + n_z, n_z), 4)
        block = rs_s.at[core, at, across]
        block_arrived(block, 1, at)
        send_block(block, block, 2, at, chip_device(z + 1))
        send_block(block, block, 3, at, chip_device(z - 1))
        send_block(block, block, 4, at, chip_device(z + 2 + 12 * lax.div(at, 2)))
        send_block(block, block, 5, at, sibling)
    sources = ((0, 0), (-1, 1), (1, 2), (-2, 3), (2, 4))
    lit_rows = [0.0] * 5
    for i in range(4):
        block = rs_s[core, i, across].astype(F32)
        for j, piece in ((0, ns_s[i, across]), (1, nr_s[0, i]), (2, nr_s[1, i]), (3 + i // 2, nr_s[2, i])):
            lit_rows[j] = lit_rows[j] + block * piece.astype(F32)
    chip = lax.broadcasted_iota(jnp.int32, (n_z, HALF), 0)
    behind = jnp.zeros((n_z, HALF), F32)
    for a, j in sources:
        row = lights[j] * jnp.sum(lit_rows[j], axis=0, keepdims=True)
        behind = behind + jnp.where(chip < lax.rem(z + a + n_z, n_z), row, 0.0)
    for i in range(n_z):
        pb[i] = behind[i:i + 1]

    def to_chip(j, n):
        to = lax.rem(z + away(j, n_z), n_z)
        pltpu.make_async_remote_copy(
            pb.at[to], rb.at[z], many_send.at[1], many_recv.at[1],
            device_id=(to, core, y, x), device_id_type=MESH).start()
        return n

    lax.fori_loop(0, n_z - 1, to_chip, 0)
    rb[z] = pb[z]

    for a in (2, -2, 6, -6):
        for i, beside, which in ((2, -1, turn(1)), (3, 1, turn(3)), (4, 2, res)):
            at = lax.div(lax.rem(z + beside + a + n_z, n_z), 4)
            block = rs_s.at[core, at, which]
            block_arrived(block, i, at)
            send_block(block, block, 4 + i, at, sibling)
    for i, which in ((5, across), (6, turn(1)), (7, turn(3)), (8, res)):
        for at in range(4):
            block_arrived(rs_s.at[other, at, which], i, at)

    transmit = tt[5]
    for half in range(2):
        block = rs_s[half].reshape(gp.shape[0], HALF).astype(F32)
        gp[:, half * HALF:(half + 1) * HALF] = (block * transmit[half:half + 1]).astype(BF16)
    q_t[...] = mm(wfb[...], gp[...])
    slopes = []
    for k in range(SAMPLES):
        slopes.append(jnp.sum(h2[k].astype(F32) * q_t[...], axis=0, keepdims=True))
    slope = jnp.concatenate(slopes, axis=0)
    lit_slope = weight * slope
    put_rows(br, core, jnp.sum(lit_slope, axis=0, keepdims=True))
    send(br.at[core], br.at[core], 7, sibling)
    gf_s[...] = nt_dot(gathered, gp[...]).astype(BF16).reshape(gf_s.shape)
    to_groups(lambda t: gf_s.at[t], gf_r, 2)

    arrived(cr_s, 6)
    first_half = jnp.where(core == 0, cp_s[core], cr_s[...])
    second_half = jnp.where(core == 0, cr_s[...], cp_s[core])
    ren_o[...] = jnp.concatenate([first_half, second_half], axis=1).astype(BF16)
    gf_r[group] = gf_s[group]
    after = jnp.sum(lit_slope, axis=0, keepdims=True) - ahead_of(lit_slope) - lit_slope
    slope_step = slope * (ahead * kept) - after
    slope_scale = travel / (1.0 + jnp.exp(-logit))

    wait_many(rb, many_recv, 1, 1)
    lp[core] = jnp.sum(rb[...], axis=0)
    send(lp.at[core], lp.at[core], 9, sibling)
    arrived(br.at[other], 7)
    follower = jnp.where(core == 0, br[1], 0.0)
    arrived(lp.at[other], 9)
    grad_depth = -jnp.concatenate([lp[0] + follower[0:1], lp[1] + follower[1:2]], axis=1)
    dg_o[...] = grad_depth
    grad_logit = (grad_depth + slope_step) * slope_scale
    for k in range(SAMPLES):
        grad = weight[k:k + 1] * q_t[...] + grad_logit[k:k + 1] * wdb[...]
        gb[:, k * n_rows:(k + 1) * n_rows] = jnp.where(h2[k].astype(F32) > 0.0, grad, 0.0).astype(BF16)
    gs_s[...] = nt_dot(h1[...], gb[...]).astype(BF16).reshape(gs_s.shape)
    to_groups(lambda t: gs_s.at[t], gs_r, 3)
    gs_r[group] = gs_s[group]

    def folded(share):
        squares = jnp.sum(share * share, axis=0, keepdims=True)
        return sum(squares[:, i:i + HALF] for i in range(0, squares.shape[1], HALF))

    wait_many(gf_r, many_recv, 2, 1)
    share_feature = jnp.sum(gf_r[...].astype(F32), axis=0)
    square_feature = folded(share_feature)
    fa_s[...] = share_feature.astype(BF16)
    to_groups(lambda t: fa_s, gf_o, 5)
    own_feature = pltpu.make_async_copy(fa_s, gf_o.at[group], loc.at[10])
    own_feature.start()
    wait_many(gs_r, many_recv, 3, 1)
    share_second = jnp.sum(gs_r[...].astype(F32), axis=0)
    sq[cell] = square_feature + folded(share_second)
    send(sq.at[cell], sq.at[cell], 8, sibling)
    to_cells(sq, 4)
    sa_s[...] = share_second.astype(BF16)
    to_groups(lambda t: sa_s, gs_o, 6)
    own_second = pltpu.make_async_copy(sa_s, gs_o.at[group], loc.at[11])
    own_second.start()
    arrived(sq.at[2 * z + other], 8)
    wait_many(sq, many_recv, 4, 2)
    sr[group] = jnp.sum(sq[...], axis=0)
    to_groups(lambda t: sr.at[group], sr, 7)
    wait_many(gf_o, many_recv, 5, 1)
    wait_many(gs_o, many_recv, 6, 1)
    own_feature.wait()
    own_second.wait()
    for copy in sent:
        copy.wait_send()
    for i, (buf, left_out) in enumerate((
        (dep, 2), (rb, 1), (gf_r, 1), (gs_r, 1), (sq, 2), (gf_o, 1), (gs_o, 1), (sr, 1),
    )):
        wait_many(buf, many_send, i, left_out)
    wait_many(sr, many_recv, 7, 1)
    sum_o[...] = jnp.sum(sr[...], axis=0)


def adam_kernel(
    entries,
    ren_h, dg_h, gs_h, gf_h, sum_h, ms_h, vs_h, mf_h, vf_h,
    ren_o, dg_o, us_o, uf_o,
    gs_v, gf_v, sum_v, ms_v, vs_v, mf_v, vf_v, us_v, uf_v,
    sem, feed, drain,
):
    n_rays, per, _ = gs_v.shape
    parts = feed.shape[0]
    groups, rows = n_rays // parts, per * n_rays // parts
    start = []
    for i, (src, dst) in enumerate(((sum_h, sum_v), (ren_h, ren_o), (dg_h, dg_o))):
        copy = pltpu.make_async_copy(src, dst, sem.at[i])
        copy.start()
        start.append(copy)
    fed = []
    for i in range(parts):
        some, block = pl.ds(i * rows, rows), pl.ds(i * groups, groups)
        copies = [
            pltpu.make_async_copy(gs_h.at[block], gs_v.at[block], feed.at[i, 0]),
            pltpu.make_async_copy(gf_h.at[block], gf_v.at[block], feed.at[i, 5]),
        ]
        for j, (src, dst) in enumerate(((ms_h, ms_v), (vs_h, vs_v), (mf_h, mf_v), (vf_h, vf_v))):
            copies.append(pltpu.make_async_copy(src.at[some], dst.at[some], feed.at[i, 1 + j]))
        for copy in copies:
            copy.start()
        fed.append(copies)
    start[0].wait()
    square_sum = jnp.sum(sum_v[...], axis=1, keepdims=True)
    rescale = lax.rsqrt(square_sum / entries + mean_floor)

    def adam(gradient, mean_moment, square_moment):
        unit = gradient.astype(F32) * rescale
        mean_new = beta_first * mean_moment + (1.0 - beta_first) * unit
        square_new = beta_second * square_moment + (1.0 - beta_second) * unit * unit
        spread = square_new * (1.0 / bias_second)
        spread = spread * lax.rsqrt(spread) + adam_floor
        return (mean_new * (1.0 / bias_first) * pltpu.reciprocal(spread)).astype(BF16)

    def update(i, n):
        at = pl.ds(pl.multiple_of(i * per, per), per)
        us_v[at, :] = adam(gs_v[i], ms_v[at, :], vs_v[at, :])
        uf_v[at, :] = adam(gf_v[i], mf_v[at, :], vf_v[at, :])
        return n

    out = []
    for i in range(parts):
        for copy in fed[i]:
            copy.wait()
        lax.fori_loop(i * groups, (i + 1) * groups, update, 0)
        some = pl.ds(i * rows, rows)
        for j, (src, dst) in enumerate(((us_v, us_o), (uf_v, uf_o))):
            out.append(pltpu.make_async_copy(src.at[some], dst.at[some], drain.at[i, j]))
            out[-1].start()
    for copy in out + start[1:]:
        copy.wait()


def on_device(sizes, ray_code, entry_index, sample_count, step_length, positions, w_first, w_second,
              w_density, w_feature, mean_second, square_second, mean_feature, square_feature, target_color):
    n_z, n_y, n_x, all_cells = sizes
    n_cell, n_rays = 2 * n_z, n_y * n_x
    rows, width = ray_code.shape[0], ray_code.shape[2]
    table, channels = positions.shape[1], target_color.shape[1]
    part = channels // 16
    per = width // n_rays
    vmem = pltpu.VMEM
    args = (
        ray_code.reshape(rows, width), entry_index.reshape(1, rows), sample_count.reshape(1, rows),
        step_length.reshape(1, rows), positions[0], w_first[0], w_second[0], w_density,
        w_feature[0], target_color,
    )
    moments = (mean_second[0], square_second[0], mean_feature[0], square_feature[0])
    local = [vmem(a.shape, a.dtype) for a in args[:-1]] + [vmem((HALF, channels), BF16)]
    scratch = local + [
        vmem((width, rows), F32), vmem((width, 2 * table), BF16),
        vmem((width, width), BF16), vmem((channels, width), BF16), vmem((width, channels), BF16),
        vmem((width, rows), F32), vmem((width, SAMPLES * rows), BF16), vmem((SAMPLES, width, rows), BF16),
        vmem((SAMPLES, rows), F32), vmem((16, part, HALF), F32), vmem((width, rows), F32),
        vmem((channels, rows), BF16), vmem((width, SAMPLES * rows), BF16),
        vmem((n_cell, 2, HALF), F32), vmem((6, 2, HALF), F32), vmem((2, 16, part, HALF), BF16),
        vmem((16, part, HALF), BF16), vmem((4, 4, part, HALF), BF16), vmem((3, 4, part, HALF), BF16),
        vmem((4, part, HALF), BF16), vmem((4, part, HALF), BF16), vmem((2, part // 2, HALF), F32),
        vmem((part // 2, HALF), F32), vmem((part, HALF), BF16), vmem((2, 4, 4, part, HALF), BF16), vmem((2, 2, HALF), F32),
        vmem((n_z, 1, HALF), F32), vmem((n_z, 1, HALF), F32), vmem((2, 1, HALF), F32),
        vmem((n_rays, per, channels), BF16), vmem((n_rays, per, channels), BF16),
        vmem((n_rays, per, width), BF16), vmem((n_rays, per, width), BF16),
        vmem((per, channels), BF16), vmem((per, width), BF16), vmem((n_cell, 1, HALF), F32), vmem((n_rays, 1, HALF), F32),
        pltpu.SemaphoreType.DMA((12,)), pltpu.SemaphoreType.DMA((8,)), pltpu.SemaphoreType.DMA((8,)),
        pltpu.SemaphoreType.DMA((10,)), pltpu.SemaphoreType.DMA((10,)),
        pltpu.SemaphoreType.DMA((36,)), pltpu.SemaphoreType.DMA((9, 4)),
    ]
    anywhere = pl.BlockSpec(memory_space=pl.ANY)
    inside = pl.BlockSpec(memory_space=vmem)
    found = pl.pallas_call(
        functools.partial(kernel, sizes),
        out_shape=(
            jax.ShapeDtypeStruct((part // 2, rows), BF16),
            jax.ShapeDtypeStruct((1, rows), F32),
            jax.ShapeDtypeStruct((n_rays, per, width), BF16),
            jax.ShapeDtypeStruct((n_rays, per, channels), BF16),
            jax.ShapeDtypeStruct((1, HALF), F32),
        ),
        in_specs=[anywhere] * len(args),
        out_specs=[inside, inside, anywhere, anywhere, inside],
        scratch_shapes=scratch,
        compiler_params=pltpu.CompilerParams(
            collective_id=0, has_side_effects=True, vmem_limit_bytes=62 * 1024 * 1024
        ),
    )(*args)
    parts = min(4, n_rays)
    rendered, depth_grad, update_second, update_feature = pl.pallas_call(
        functools.partial(adam_kernel, all_cells * width * (width + channels)),
        out_shape=(
            jax.ShapeDtypeStruct((part // 2, rows), BF16),
            jax.ShapeDtypeStruct((1, rows), F32),
            jax.ShapeDtypeStruct((width, width), BF16),
            jax.ShapeDtypeStruct((width, channels), BF16),
        ),
        in_specs=[anywhere] * 9,
        out_specs=[anywhere] * 4,
        scratch_shapes=[
            vmem((n_rays, per, width), BF16), vmem((n_rays, per, channels), BF16), vmem((1, HALF), F32),
            *(vmem(m.shape, F32) for m in moments),
            vmem((width, width), BF16), vmem((width, channels), BF16),
            pltpu.SemaphoreType.DMA((3,)), pltpu.SemaphoreType.DMA((parts, 6)), pltpu.SemaphoreType.DMA((parts, 2)),
        ],
        compiler_params=pltpu.CompilerParams(vmem_limit_bytes=62 * 1024 * 1024),
    )(*found, *moments)
    return (rendered.T, depth_grad.reshape(rows, 1), update_second[None], update_feature[None])


def solution(mesh):
    n_cell, n_rays = mesh.devices.shape
    n_y = 4 if n_rays == 16 else 1
    sizes = (n_cell // 2, n_y, n_rays // n_y, n_cell)
    split = Mesh(mesh.devices.reshape(n_cell // 2, 2, n_y, n_rays // n_y), ("z", "core", "y", "x"))
    return jax.shard_map(
        functools.partial(on_device, sizes),
        mesh=split,
        in_specs=(
            P(RAYS, CELL, None),
            P(RAYS, CELL),
            P(RAYS, CELL),
            P(RAYS, CELL),
            P(CELL, None, None),
            P(CELL, None, None),
            P(CELL, None, None),
            P(CELL, None),
            P(CELL, None, None),
            P(CELL, None, None),
            P(CELL, None, None),
            P(CELL, None, None),
            P(CELL, None, None),
            P(RAYS, None),
        ),
        out_specs=(P(RAYS, CELL), P(RAYS, CELL), P(CELL, None, None), P(CELL, None, None)),
        check_vma=False,
    )
```

```python
import functools

import jax
import jax.numpy as jnp
from jax import lax
from jax.experimental import pallas as pl
from jax.experimental.pallas import tpu as pltpu
from jax.sharding import Mesh
from jax.sharding import PartitionSpec as P

SAMPLES = 8
MESH = pl.DeviceIdType.MESH
CELL = ("z", "core")
RAYS = ("y", "x")
HALF = 128
F32 = jnp.float32
BF16 = jnp.bfloat16

beta_first = 0.9
beta_second = 0.999
bias_first = 0.19
bias_second = 0.001999
adam_floor = 1e-08
mean_floor = 1e-06


def nt_dot(a, b):
    return lax.dot_general(a, b, (((1,), (1,)), ((), ())), preferred_element_type=F32)


def mm(a, b):
    return jnp.dot(a, b, preferred_element_type=F32)


def kernel(
    sizes,
    ray_h, ent_h, cnt_h, stp_h, pos_h, w1_h, w2_h, wd_h, wf_h,
    tgt_h,
    ren_o, dg_o, gs_o, gf_o, sum_o,
    ray_v, ent_v, cnt_v, stp_v, pos_v, w1_v, w2_v, wd_v, wf_v,
    tgt_v,
    rayt, post, w2t, wft, wfb, wdb, h1, h2, lg, tgt_t, q_t, gp, gb,
    dep, tt, pl_s, pr_s, ns_s, nr_s, fs_s, fr_s, cp_s, cr_s, own_s, rs_s, br, pb, rb, lp,
    gf_s, gf_r, gs_s, gs_r, fa_s, sa_s, sq, sr,
    loc, many_send, many_recv, one_send, one_recv, blk_send, blk_recv,
):
    n_z, n_y, n_x, _ = sizes
    n_cell, n_rays = 2 * n_z, n_y * n_x
    z, core = lax.axis_index("z"), lax.axis_index("core")
    y, x = lax.axis_index("y"), lax.axis_index("x")
    cell = 2 * z + core
    group = n_x * y + x
    quad, res = lax.div(z, 4), lax.rem(z, 4)
    other = 1 - core

    def cell_device(t):
        return (lax.div(t, 2), lax.rem(t, 2), y, x)

    def rays_device(t):
        return (z, core, lax.div(t, n_x), lax.rem(t, n_x))

    def chip_device(t):
        return (lax.rem(t + n_z, n_z), core, y, x)

    sibling = (z, other, y, x)

    def away(i, n):
        half = lax.div(i + 1, 2)
        return n // 2 + half - 2 * half * lax.rem(i, 2)

    def each_cell(send):
        def step(j, n):
            send(2 * lax.rem(z + away(lax.div(j, 2), n_z), n_z) + lax.rem(j, 2))
            return n

        lax.fori_loop(0, n_cell - 2, step, 0)

    def each_group(send):
        def step(j, n):
            to_y = lax.rem(y + away(lax.div(j, n_x), n_y), n_y)
            to_x = lax.rem(x + away(lax.rem(j, n_x), n_x), n_x)
            send(to_y * n_x + to_x)
            return n

        lax.fori_loop(0, n_rays - 1, step, 0)

    bring = {}
    for i, (name, src, dst) in enumerate((
        ("ent", ent_h, ent_v), ("pos", pos_h, pos_v), ("ray", ray_h, ray_v), ("w1", w1_h, w1_v),
        ("w2", w2_h, w2_v), ("wd", wd_h, wd_v), ("cnt", cnt_h, cnt_v), ("stp", stp_h, stp_v),
        ("wf", wf_h, wf_v),
        ("tgt", tgt_h.at[pl.ds(pl.multiple_of(core * HALF, HALF), HALF), :], tgt_v),
    )):
        bring[name] = pltpu.make_async_copy(src, dst, loc.at[i])
        bring[name].start()

    barrier = pltpu.get_barrier_semaphore()
    each_cell(lambda t: pl.semaphore_signal(barrier, inc=1, device_id=cell_device(t), device_id_type=MESH))
    pl.semaphore_signal(barrier, inc=1, device_id=sibling, device_id_type=MESH)
    each_group(lambda t: pl.semaphore_signal(barrier, inc=1, device_id=rays_device(t), device_id_type=MESH))

    for name in ("pos", "ray", "w1"):
        bring[name].wait()
    width = wd_v.shape[1]
    n_rows = ray_v.shape[0]
    placed = mm(pos_v[...], w1_v[...]).T
    coarse = placed.astype(BF16)
    post[...] = jnp.concatenate([coarse, (placed - coarse.astype(F32)).astype(BF16)], axis=1)
    rayt[...] = mm(ray_v[...], w1_v[...]).T
    for name in ("w2", "wd", "ent", "cnt", "stp", "wf"):
        bring[name].wait()
    w2t[...] = w2_v[...].T.astype(BF16)
    column = jnp.broadcast_to(wd_v[...].astype(F32), (HALF, width)).T
    wdb[...] = jnp.concatenate([column] * (n_rows // HALF), axis=1)
    slot = lax.broadcasted_iota(jnp.int32, (pos_v.shape[0], n_rows), 0)
    for k in range(SAMPLES):
        hot = jnp.where(slot == ent_v[...] + k, 1.0, 0.0).astype(BF16)
        hot = jnp.concatenate([hot, hot], axis=0)
        first = jnp.maximum(mm(post[...], hot) + rayt[...], 0.0).astype(BF16)
        second = jnp.maximum(mm(w2t[...], first), 0.0).astype(BF16)
        h1[:, k * n_rows:(k + 1) * n_rows] = first
        h2[k] = second
        lg[k:k + 1] = jnp.sum(second.astype(F32) * wdb[...], axis=0, keepdims=True)

    order = lax.broadcasted_iota(jnp.int32, (SAMPLES, n_rows), 0)
    logit = lg[...]
    travel = jnp.where(order < cnt_v[...], stp_v[...], 0.0)
    step_depth = (jnp.maximum(logit, 0.0) + jnp.log1p(jnp.exp(-jnp.abs(logit)))) * travel

    def ahead_of(v):
        total = v
        for shift in (1, 2, 4):
            total = total + jnp.where(order >= shift, pltpu.roll(total, shift, 0), 0.0)
        return total - v

    ahead = jnp.exp(-ahead_of(step_depth))
    kept = jnp.exp(-step_depth)
    weight = ahead * (1.0 - kept)
    depth = jnp.sum(step_depth, axis=0, keepdims=True)

    def put_rows(buf, at, row):
        for half in range(2):
            buf[at, pl.ds(half, 1), :] = row[:, half * HALF:(half + 1) * HALF]

    put_rows(dep, cell, depth)
    pl.semaphore_wait(barrier, n_cell - 1 + n_rays - 1)

    def to_cells(buf, i):
        each_cell(lambda t: pltpu.make_async_remote_copy(
            buf.at[cell], buf.at[cell], many_send.at[i], many_recv.at[i],
            device_id=cell_device(t), device_id_type=MESH).start())

    def to_groups(src, dst, i):
        each_group(lambda t: pltpu.make_async_remote_copy(
            src(t), dst.at[group], many_send.at[i], many_recv.at[i],
            device_id=rays_device(t), device_id_type=MESH).start())

    def wait_many(buf, sem, i, left_out):
        part = buf.at[pl.ds(0, buf.shape[0] - left_out)]
        pltpu.make_async_copy(part, part, sem.at[i]).wait()

    sent, blocks = [], []

    def send(src, dst, i, device):
        copy = pltpu.make_async_remote_copy(
            src, dst, one_send.at[i], one_recv.at[i], device_id=device, device_id_type=MESH)
        copy.start()
        sent.append(copy)

    def arrived(dst, i):
        pltpu.make_async_copy(dst, dst, one_recv.at[i]).wait()

    def send_block(src, dst, i, at, device):
        copy = pltpu.make_async_remote_copy(
            src, dst, blk_send.at[len(blocks)], blk_recv.at[i, at], device_id=device, device_id_type=MESH)
        copy.start()
        sent.append(copy)
        blocks.append(copy)

    def block_arrived(dst, i, at):
        pltpu.make_async_copy(dst, dst, blk_recv.at[i, at]).wait()

    send(dep.at[cell], dep.at[cell], 5, sibling)
    to_cells(dep, 0)

    gather = weight[0:1] * h2[0].astype(F32)
    for k in range(1, SAMPLES):
        gather = gather + weight[k:k + 1] * h2[k].astype(F32)
    gathered = gather.astype(BF16)
    wfb[...] = wf_v[...].astype(BF16)
    wft[...] = wf_v[...].T.astype(BF16)
    partial = mm(wft[...], gathered).astype(BF16)
    for half in range(2):
        pl_s[half] = partial[:, half * HALF:(half + 1) * HALF].reshape(pl_s.shape[1:])
    send(pl_s.at[other], pr_s, 0, sibling)

    arrived(dep.at[2 * z + other], 5)
    nearer = jnp.exp(-dep[2 * z, pl.ds(core, 1), :])
    mine = jnp.where(core == 0, 1.0, nearer)
    theirs = jnp.where(core == 0, nearer, 1.0)
    arrived(pr_s, 0)
    for i in range(16):
        ns_s[i // 4, i % 4] = (mine * pl_s[core, i].astype(F32) + theirs * pr_s[i].astype(F32)).astype(BF16)

    def turn(a):
        return lax.rem(res + a + 4, 4)

    across = turn(2)
    send(ns_s.at[pl.ds(0, 2), res], nr_s.at[2, pl.ds(0, 2)], 3, chip_device(z + 2))
    send(ns_s.at[pl.ds(2, 2), res], nr_s.at[2, pl.ds(2, 2)], 4, chip_device(z - 2))
    send(ns_s.at[:, turn(3)], nr_s.at[0], 1, chip_device(z + 1))
    send(ns_s.at[:, turn(1)], nr_s.at[1], 2, chip_device(z - 1))
    bring["tgt"].wait()
    tgt_t[...] = tgt_v[...].astype(F32).T.reshape(tgt_t.shape)

    wait_many(dep, many_recv, 0, 2)
    number = lax.broadcasted_iota(jnp.int32, dep.shape, 0)
    depths = dep[...]

    def light(end):
        return jnp.exp(-jnp.sum(jnp.where(number < end, depths, 0.0), axis=0))

    for i, a in enumerate((0, -1, 1, -2, 2)):
        tt[i] = light(2 * lax.rem(z + a + n_z, n_z))
    tt[5] = light(cell)
    lights = [tt[i, pl.ds(core, 1), :] for i in range(5)]
    arrived(nr_s.at[0], 1)
    arrived(nr_s.at[1], 2)
    arrived(nr_s.at[2, pl.ds(0, 2)], 3)
    arrived(nr_s.at[2, pl.ds(2, 2)], 4)
    for i in range(4):
        fs_s[i] = (
            lights[0] * ns_s[i, across].astype(F32) + lights[1] * nr_s[0, i].astype(F32)
            + lights[2] * nr_s[1, i].astype(F32) + lights[3 + i // 2] * nr_s[2, i].astype(F32)
        ).astype(BF16)
    for a in (6, -6, 2, -2):
        to = lax.rem(z + a + n_z, n_z)
        send_block(fs_s.at[lax.div(to, 4)], fr_s.at[quad], 0, quad, chip_device(to))
    for i in range(4):
        block_arrived(fr_s.at[i], 0, i)
    lit = fr_s[0].astype(F32) + fr_s[1].astype(F32) + fr_s[2].astype(F32) + fr_s[3].astype(F32)

    own_s[...] = (lit - tgt_t[z]).astype(BF16)
    for a in (6, -6, 2, -2):
        send_block(own_s, rs_s.at[core, quad, res], 1, quad, chip_device(z + a + n_z))
    cp_s[...] = lit.reshape(cp_s.shape)
    send(cp_s.at[other], cr_s, 6, sibling)
    for a in (2, -2, 6, -6):
        at = lax.div(lax.rem(z + a + n_z, n_z), 4)
        block = rs_s.at[core, at, across]
        block_arrived(block, 1, at)
        send_block(block, block, 4, at, chip_device(z + 2 + 12 * lax.div(at, 2)))
        send_block(block, block, 2, at, chip_device(z + 1))
        send_block(block, block, 3, at, chip_device(z - 1))
        send_block(block, block, 5, at, sibling)
    sources = ((0, 0), (-1, 1), (1, 2), (-2, 3), (2, 4))
    lit_rows = [0.0] * 5
    for i in range(4):
        block = rs_s[core, i, across].astype(F32)
        for j, piece in ((0, ns_s[i, across]), (1, nr_s[0, i]), (2, nr_s[1, i]), (3 + i // 2, nr_s[2, i])):
            lit_rows[j] = lit_rows[j] + block * piece.astype(F32)
    chip = lax.broadcasted_iota(jnp.int32, (n_z, HALF), 0)
    behind = jnp.zeros((n_z, HALF), F32)
    for a, j in sources:
        row = lights[j] * jnp.sum(lit_rows[j], axis=0, keepdims=True)
        behind = behind + jnp.where(chip < lax.rem(z + a + n_z, n_z), row, 0.0)
    for i in range(n_z):
        pb[i] = behind[i:i + 1]

    def to_chip(j, n):
        to = lax.rem(z + away(j, n_z), n_z)
        pltpu.make_async_remote_copy(
            pb.at[to], rb.at[z], many_send.at[1], many_recv.at[1],
            device_id=(to, core, y, x), device_id_type=MESH).start()
        return n

    lax.fori_loop(0, n_z - 1, to_chip, 0)
    rb[z] = pb[z]

    for a in (2, -2, 6, -6):
        for i, beside, which in ((2, -1, turn(1)), (3, 1, turn(3)), (4, 2, res)):
            at = lax.div(lax.rem(z + beside + a + n_z, n_z), 4)
            block = rs_s.at[core, at, which]
            block_arrived(block, i, at)
            send_block(block, block, 4 + i, at, sibling)
    for i, which in ((5, across), (6, turn(1)), (7, turn(3)), (8, res)):
        for at in range(4):
            block_arrived(rs_s.at[other, at, which], i, at)

    transmit = tt[5]
    for half in range(2):
        block = rs_s[half].reshape(gp.shape[0], HALF).astype(F32)
        gp[:, half * HALF:(half + 1) * HALF] = (block * transmit[half:half + 1]).astype(BF16)
    q_t[...] = mm(wfb[...], gp[...])
    slopes = []
    for k in range(SAMPLES):
        slopes.append(jnp.sum(h2[k].astype(F32) * q_t[...], axis=0, keepdims=True))
    slope = jnp.concatenate(slopes, axis=0)
    lit_slope = weight * slope
    put_rows(br, core, jnp.sum(lit_slope, axis=0, keepdims=True))
    send(br.at[core], br.at[core], 7, sibling)
    gf_s[...] = nt_dot(gathered, gp[...]).astype(BF16).reshape(gf_s.shape)
    to_groups(lambda t: gf_s.at[t], gf_r, 2)

    arrived(cr_s, 6)
    first_half = jnp.where(core == 0, cp_s[core], cr_s[...])
    second_half = jnp.where(core == 0, cr_s[...], cp_s[core])
    ren_o[...] = jnp.concatenate([first_half, second_half], axis=1).astype(BF16)
    gf_r[group] = gf_s[group]
    after = jnp.sum(lit_slope, axis=0, keepdims=True) - ahead_of(lit_slope) - lit_slope
    slope_step = slope * (ahead * kept) - after
    slope_scale = travel / (1.0 + jnp.exp(-logit))

    wait_many(rb, many_recv, 1, 1)
    lp[core] = jnp.sum(rb[...], axis=0)
    send(lp.at[core], lp.at[core], 9, sibling)
    arrived(br.at[other], 7)
    follower = jnp.where(core == 0, br[1], 0.0)
    arrived(lp.at[other], 9)
    grad_depth = -jnp.concatenate([lp[0] + follower[0:1], lp[1] + follower[1:2]], axis=1)
    dg_o[...] = grad_depth
    grad_logit = (grad_depth + slope_step) * slope_scale
    for k in range(SAMPLES):
        grad = weight[k:k + 1] * q_t[...] + grad_logit[k:k + 1] * wdb[...]
        gb[:, k * n_rows:(k + 1) * n_rows] = jnp.where(h2[k].astype(F32) > 0.0, grad, 0.0).astype(BF16)
    gs_s[...] = nt_dot(h1[...], gb[...]).astype(BF16).reshape(gs_s.shape)
    to_groups(lambda t: gs_s.at[t], gs_r, 3)
    gs_r[group] = gs_s[group]

    def folded(share):
        squares = jnp.sum(share * share, axis=0, keepdims=True)
        return sum(squares[:, i:i + HALF] for i in range(0, squares.shape[1], HALF))

    wait_many(gf_r, many_recv, 2, 1)
    share_feature = jnp.sum(gf_r[...].astype(F32), axis=0)
    square_feature = folded(share_feature)
    fa_s[...] = share_feature.astype(BF16)
    to_groups(lambda t: fa_s, gf_o, 5)
    own_feature = pltpu.make_async_copy(fa_s, gf_o.at[group], loc.at[10])
    own_feature.start()
    wait_many(gs_r, many_recv, 3, 1)
    share_second = jnp.sum(gs_r[...].astype(F32), axis=0)
    sq[cell] = square_feature + folded(share_second)
    send(sq.at[cell], sq.at[cell], 8, sibling)
    to_cells(sq, 4)
    sa_s[...] = share_second.astype(BF16)
    to_groups(lambda t: sa_s, gs_o, 6)
    own_second = pltpu.make_async_copy(sa_s, gs_o.at[group], loc.at[11])
    own_second.start()
    arrived(sq.at[2 * z + other], 8)
    wait_many(sq, many_recv, 4, 2)
    sr[group] = jnp.sum(sq[...], axis=0)
    to_groups(lambda t: sr.at[group], sr, 7)
    wait_many(gf_o, many_recv, 5, 1)
    wait_many(gs_o, many_recv, 6, 1)
    own_feature.wait()
    own_second.wait()
    for copy in sent:
        copy.wait_send()
    for i, (buf, left_out) in enumerate((
        (dep, 2), (rb, 1), (gf_r, 1), (gs_r, 1), (sq, 2), (gf_o, 1), (gs_o, 1), (sr, 1),
    )):
        wait_many(buf, many_send, i, left_out)
    wait_many(sr, many_recv, 7, 1)
    sum_o[...] = jnp.sum(sr[...], axis=0)


def adam_kernel(
    entries,
    ren_h, dg_h, gs_h, gf_h, sum_h, ms_h, vs_h, mf_h, vf_h,
    ren_o, dg_o, us_o, uf_o,
    gs_v, gf_v, sum_v, ms_v, vs_v, mf_v, vf_v, us_v, uf_v,
    sem, feed, drain,
):
    n_rays, per, _ = gs_v.shape
    parts = feed.shape[0]
    groups, rows = n_rays // parts, per * n_rays // parts
    start = []
    for i, (src, dst) in enumerate(((sum_h, sum_v), (ren_h, ren_o), (dg_h, dg_o))):
        copy = pltpu.make_async_copy(src, dst, sem.at[i])
        copy.start()
        start.append(copy)
    fed = []
    for i in range(parts):
        some, block = pl.ds(i * rows, rows), pl.ds(i * groups, groups)
        copies = [
            pltpu.make_async_copy(gs_h.at[block], gs_v.at[block], feed.at[i, 0]),
            pltpu.make_async_copy(gf_h.at[block], gf_v.at[block], feed.at[i, 5]),
        ]
        for j, (src, dst) in enumerate(((ms_h, ms_v), (vs_h, vs_v), (mf_h, mf_v), (vf_h, vf_v))):
            copies.append(pltpu.make_async_copy(src.at[some], dst.at[some], feed.at[i, 1 + j]))
        for copy in copies:
            copy.start()
        fed.append(copies)
    start[0].wait()
    square_sum = jnp.sum(sum_v[...], axis=1, keepdims=True)
    rescale = lax.rsqrt(square_sum / entries + mean_floor)

    def adam(gradient, mean_moment, square_moment):
        unit = gradient.astype(F32) * rescale
        mean_new = beta_first * mean_moment + (1.0 - beta_first) * unit
        square_new = beta_second * square_moment + (1.0 - beta_second) * unit * unit
        spread = square_new * (1.0 / bias_second)
        spread = spread * lax.rsqrt(spread) + adam_floor
        return (mean_new * (1.0 / bias_first) * pltpu.reciprocal(spread)).astype(BF16)

    def update(i, n):
        at = pl.ds(pl.multiple_of(i * per, per), per)
        us_v[at, :] = adam(gs_v[i], ms_v[at, :], vs_v[at, :])
        uf_v[at, :] = adam(gf_v[i], mf_v[at, :], vf_v[at, :])
        return n

    out = []
    for i in range(parts):
        for copy in fed[i]:
            copy.wait()
        lax.fori_loop(i * groups, (i + 1) * groups, update, 0)
        some = pl.ds(i * rows, rows)
        for j, (src, dst) in enumerate(((us_v, us_o), (uf_v, uf_o))):
            out.append(pltpu.make_async_copy(src.at[some], dst.at[some], drain.at[i, j]))
            out[-1].start()
    for copy in out + start[1:]:
        copy.wait()


def on_device(sizes, ray_code, entry_index, sample_count, step_length, positions, w_first, w_second,
              w_density, w_feature, mean_second, square_second, mean_feature, square_feature, target_color):
    n_z, n_y, n_x, all_cells = sizes
    n_cell, n_rays = 2 * n_z, n_y * n_x
    rows, width = ray_code.shape[0], ray_code.shape[2]
    table, channels = positions.shape[1], target_color.shape[1]
    part = channels // 16
    per = width // n_rays
    vmem = pltpu.VMEM
    args = (
        ray_code.reshape(rows, width), entry_index.reshape(1, rows), sample_count.reshape(1, rows),
        step_length.reshape(1, rows), positions[0], w_first[0], w_second[0], w_density,
        w_feature[0], target_color,
    )
    moments = (mean_second[0], square_second[0], mean_feature[0], square_feature[0])
    local = [vmem(a.shape, a.dtype) for a in args[:-1]] + [vmem((HALF, channels), BF16)]
    scratch = local + [
        vmem((width, rows), F32), vmem((width, 2 * table), BF16),
        vmem((width, width), BF16), vmem((channels, width), BF16), vmem((width, channels), BF16),
        vmem((width, rows), F32), vmem((width, SAMPLES * rows), BF16), vmem((SAMPLES, width, rows), BF16),
        vmem((SAMPLES, rows), F32), vmem((16, part, HALF), F32), vmem((width, rows), F32),
        vmem((channels, rows), BF16), vmem((width, SAMPLES * rows), BF16),
        vmem((n_cell, 2, HALF), F32), vmem((6, 2, HALF), F32), vmem((2, 16, part, HALF), BF16),
        vmem((16, part, HALF), BF16), vmem((4, 4, part, HALF), BF16), vmem((3, 4, part, HALF), BF16),
        vmem((4, part, HALF), BF16), vmem((4, part, HALF), BF16), vmem((2, part // 2, HALF), F32),
        vmem((part // 2, HALF), F32), vmem((part, HALF), BF16), vmem((2, 4, 4, part, HALF), BF16), vmem((2, 2, HALF), F32),
        vmem((n_z, 1, HALF), F32), vmem((n_z, 1, HALF), F32), vmem((2, 1, HALF), F32),
        vmem((n_rays, per, channels), BF16), vmem((n_rays, per, channels), BF16),
        vmem((n_rays, per, width), BF16), vmem((n_rays, per, width), BF16),
        vmem((per, channels), BF16), vmem((per, width), BF16), vmem((n_cell, 1, HALF), F32), vmem((n_rays, 1, HALF), F32),
        pltpu.SemaphoreType.DMA((12,)), pltpu.SemaphoreType.DMA((8,)), pltpu.SemaphoreType.DMA((8,)),
        pltpu.SemaphoreType.DMA((10,)), pltpu.SemaphoreType.DMA((10,)),
        pltpu.SemaphoreType.DMA((36,)), pltpu.SemaphoreType.DMA((9, 4)),
    ]
    anywhere = pl.BlockSpec(memory_space=pl.ANY)
    inside = pl.BlockSpec(memory_space=vmem)
    found = pl.pallas_call(
        functools.partial(kernel, sizes),
        out_shape=(
            jax.ShapeDtypeStruct((part // 2, rows), BF16),
            jax.ShapeDtypeStruct((1, rows), F32),
            jax.ShapeDtypeStruct((n_rays, per, width), BF16),
            jax.ShapeDtypeStruct((n_rays, per, channels), BF16),
            jax.ShapeDtypeStruct((1, HALF), F32),
        ),
        in_specs=[anywhere] * len(args),
        out_specs=[inside, inside, anywhere, anywhere, inside],
        scratch_shapes=scratch,
        compiler_params=pltpu.CompilerParams(
            collective_id=0, has_side_effects=True, vmem_limit_bytes=62 * 1024 * 1024
        ),
    )(*args)
    parts = min(4, n_rays)
    rendered, depth_grad, update_second, update_feature = pl.pallas_call(
        functools.partial(adam_kernel, all_cells * width * (width + channels)),
        out_shape=(
            jax.ShapeDtypeStruct((part // 2, rows), BF16),
            jax.ShapeDtypeStruct((1, rows), F32),
            jax.ShapeDtypeStruct((width, width), BF16),
            jax.ShapeDtypeStruct((width, channels), BF16),
        ),
        in_specs=[anywhere] * 9,
        out_specs=[anywhere] * 4,
        scratch_shapes=[
            vmem((n_rays, per, width), BF16), vmem((n_rays, per, channels), BF16), vmem((1, HALF), F32),
            *(vmem(m.shape, F32) for m in moments),
            vmem((width, width), BF16), vmem((width, channels), BF16),
            pltpu.SemaphoreType.DMA((3,)), pltpu.SemaphoreType.DMA((parts, 6)), pltpu.SemaphoreType.DMA((parts, 2)),
        ],
        compiler_params=pltpu.CompilerParams(vmem_limit_bytes=62 * 1024 * 1024),
    )(*found, *moments)
    return (rendered.T, depth_grad.reshape(rows, 1), update_second[None], update_feature[None])


def solution(mesh):
    n_cell, n_rays = mesh.devices.shape
    n_y = 4 if n_rays == 16 else 1
    sizes = (n_cell // 2, n_y, n_rays // n_y, n_cell)
    split = Mesh(mesh.devices.reshape(n_cell // 2, 2, n_y, n_rays // n_y), ("z", "core", "y", "x"))
    return jax.shard_map(
        functools.partial(on_device, sizes),
        mesh=split,
        in_specs=(
            P(RAYS, CELL, None),
            P(RAYS, CELL),
            P(RAYS, CELL),
            P(RAYS, CELL),
            P(CELL, None, None),
            P(CELL, None, None),
            P(CELL, None, None),
            P(CELL, None),
            P(CELL, None, None),
            P(CELL, None, None),
            P(CELL, None, None),
            P(CELL, None, None),
            P(CELL, None, None),
            P(RAYS, None),
        ),
        out_specs=(P(RAYS, CELL), P(RAYS, CELL), P(CELL, None, None), P(CELL, None, None)),
        check_vma=False,
    )
```

```python
import functools

import jax
import jax.numpy as jnp
from jax import lax
from jax.experimental import pallas as pl
from jax.experimental.pallas import tpu as pltpu
from jax.sharding import Mesh
from jax.sharding import PartitionSpec as P

SAMPLES = 8
MESH = pl.DeviceIdType.MESH
CELL = ("z", "core")
RAYS = ("y", "x")
HALF = 128
F32 = jnp.float32
BF16 = jnp.bfloat16

beta_first = 0.9
beta_second = 0.999
bias_first = 0.19
bias_second = 0.001999
adam_floor = 1e-08
mean_floor = 1e-06


def nt_dot(a, b):
    return lax.dot_general(a, b, (((1,), (1,)), ((), ())), preferred_element_type=F32)


def mm(a, b):
    return jnp.dot(a, b, preferred_element_type=F32)


def kernel(
    sizes,
    ray_h, ent_h, cnt_h, stp_h, pos_h, w1_h, w2_h, wd_h, wf_h,
    tgt_h,
    ren_o, dg_o, gs_o, gf_o, sum_o,
    ray_v, ent_v, cnt_v, stp_v, pos_v, w1_v, w2_v, wd_v, wf_v,
    tgt_v,
    rayt, post, w2t, wft, wfb, wdb, h1, h2, lg, tgt_t, q_t, gp, gb,
    dep, tt, pl_s, pr_s, ns_s, nr_s, fs_s, fr_s, cp_s, cr_s, own_s, rs_s, br, pb, rb, lp,
    gf_s, gf_r, gs_s, gs_r, fa_s, sa_s, sq, sr,
    loc, many_send, many_recv, one_send, one_recv, blk_send, blk_recv,
):
    n_z, n_y, n_x, _ = sizes
    n_cell, n_rays = 2 * n_z, n_y * n_x
    z, core = lax.axis_index("z"), lax.axis_index("core")
    y, x = lax.axis_index("y"), lax.axis_index("x")
    cell = 2 * z + core
    group = n_x * y + x
    quad, res = lax.div(z, 4), lax.rem(z, 4)
    other = 1 - core

    def cell_device(t):
        return (lax.div(t, 2), lax.rem(t, 2), y, x)

    def rays_device(t):
        return (z, core, lax.div(t, n_x), lax.rem(t, n_x))

    def chip_device(t):
        return (lax.rem(t + n_z, n_z), core, y, x)

    sibling = (z, other, y, x)

    def away(i, n):
        half = lax.div(i + 1, 2)
        return n // 2 + half - 2 * half * lax.rem(i, 2)

    def each_cell(send):
        def step(j, n):
            send(2 * lax.rem(z + away(lax.div(j, 2), n_z), n_z) + lax.rem(j, 2))
            return n

        lax.fori_loop(0, n_cell - 2, step, 0)

    def each_group(send):
        def step(j, n):
            to_y = lax.rem(y + away(lax.div(j, n_x), n_y), n_y)
            to_x = lax.rem(x + away(lax.rem(j, n_x), n_x), n_x)
            send(to_y * n_x + to_x)
            return n

        lax.fori_loop(0, n_rays - 1, step, 0)

    bring = {}
    for i, (name, src, dst) in enumerate((
        ("ent", ent_h, ent_v), ("pos", pos_h, pos_v), ("ray", ray_h, ray_v), ("w1", w1_h, w1_v),
        ("w2", w2_h, w2_v), ("wd", wd_h, wd_v), ("cnt", cnt_h, cnt_v), ("stp", stp_h, stp_v),
        ("wf", wf_h, wf_v),
        ("tgt", tgt_h.at[pl.ds(pl.multiple_of(core * HALF, HALF), HALF), :], tgt_v),
    )):
        bring[name] = pltpu.make_async_copy(src, dst, loc.at[i])
        bring[name].start()

    barrier = pltpu.get_barrier_semaphore()
    each_cell(lambda t: pl.semaphore_signal(barrier, inc=1, device_id=cell_device(t), device_id_type=MESH))
    pl.semaphore_signal(barrier, inc=1, device_id=sibling, device_id_type=MESH)
    each_group(lambda t: pl.semaphore_signal(barrier, inc=1, device_id=rays_device(t), device_id_type=MESH))

    for name in ("pos", "ray", "w1"):
        bring[name].wait()
    width = wd_v.shape[1]
    n_rows = ray_v.shape[0]
    placed = mm(pos_v[...], w1_v[...]).T
    coarse = placed.astype(BF16)
    post[...] = jnp.concatenate([coarse, (placed - coarse.astype(F32)).astype(BF16)], axis=1)
    rayt[...] = mm(ray_v[...], w1_v[...]).T
    for name in ("w2", "wd", "ent", "cnt", "stp", "wf"):
        bring[name].wait()
    w2t[...] = w2_v[...].T.astype(BF16)
    column = jnp.broadcast_to(wd_v[...].astype(F32), (HALF, width)).T
    wdb[...] = jnp.concatenate([column] * (n_rows // HALF), axis=1)
    slot = lax.broadcasted_iota(jnp.int32, (pos_v.shape[0], n_rows), 0)
    for k in range(SAMPLES):
        hot = jnp.where(slot == ent_v[...] + k, 1.0, 0.0).astype(BF16)
        hot = jnp.concatenate([hot, hot], axis=0)
        first = jnp.maximum(mm(post[...], hot) + rayt[...], 0.0).astype(BF16)
        second = jnp.maximum(mm(w2t[...], first), 0.0).astype(BF16)
        h1[:, k * n_rows:(k + 1) * n_rows] = first
        h2[k] = second
        lg[k:k + 1] = jnp.sum(second.astype(F32) * wdb[...], axis=0, keepdims=True)

    order = lax.broadcasted_iota(jnp.int32, (SAMPLES, n_rows), 0)
    logit = lg[...]
    travel = jnp.where(order < cnt_v[...], stp_v[...], 0.0)
    step_depth = (jnp.maximum(logit, 0.0) + jnp.log1p(jnp.exp(-jnp.abs(logit)))) * travel

    def ahead_of(v):
        total = v
        for shift in (1, 2, 4):
            total = total + jnp.where(order >= shift, pltpu.roll(total, shift, 0), 0.0)
        return total - v

    ahead = jnp.exp(-ahead_of(step_depth))
    kept = jnp.exp(-step_depth)
    weight = ahead * (1.0 - kept)
    depth = jnp.sum(step_depth, axis=0, keepdims=True)

    def put_rows(buf, at, row):
        for half in range(2):
            buf[at, pl.ds(half, 1), :] = row[:, half * HALF:(half + 1) * HALF]

    put_rows(dep, cell, depth)
    pl.semaphore_wait(barrier, n_cell - 1 + n_rays - 1)

    def to_cells(buf, i):
        each_cell(lambda t: pltpu.make_async_remote_copy(
            buf.at[cell], buf.at[cell], many_send.at[i], many_recv.at[i],
            device_id=cell_device(t), device_id_type=MESH).start())

    def to_groups(src, dst, i):
        each_group(lambda t: pltpu.make_async_remote_copy(
            src(t), dst.at[group], many_send.at[i], many_recv.at[i],
            device_id=rays_device(t), device_id_type=MESH).start())

    def wait_many(buf, sem, i, left_out):
        part = buf.at[pl.ds(0, buf.shape[0] - left_out)]
        pltpu.make_async_copy(part, part, sem.at[i]).wait()

    sent, blocks = [], []

    def send(src, dst, i, device):
        copy = pltpu.make_async_remote_copy(
            src, dst, one_send.at[i], one_recv.at[i], device_id=device, device_id_type=MESH)
        copy.start()
        sent.append(copy)

    def arrived(dst, i):
        pltpu.make_async_copy(dst, dst, one_recv.at[i]).wait()

    def send_block(src, dst, i, at, device):
        copy = pltpu.make_async_remote_copy(
            src, dst, blk_send.at[len(blocks)], blk_recv.at[i, at], device_id=device, device_id_type=MESH)
        copy.start()
        sent.append(copy)
        blocks.append(copy)

    def block_arrived(dst, i, at):
        pltpu.make_async_copy(dst, dst, blk_recv.at[i, at]).wait()

    send(dep.at[cell], dep.at[cell], 5, sibling)
    to_cells(dep, 0)

    gather = weight[0:1] * h2[0].astype(F32)
    for k in range(1, SAMPLES):
        gather = gather + weight[k:k + 1] * h2[k].astype(F32)
    gathered = gather.astype(BF16)
    wfb[...] = wf_v[...].astype(BF16)
    wft[...] = wf_v[...].T.astype(BF16)
    partial = mm(wft[...], gathered).astype(BF16)
    for half in range(2):
        pl_s[half] = partial[:, half * HALF:(half + 1) * HALF].reshape(pl_s.shape[1:])
    send(pl_s.at[other], pr_s, 0, sibling)

    arrived(dep.at[2 * z + other], 5)
    nearer = jnp.exp(-dep[2 * z, pl.ds(core, 1), :])
    mine = jnp.where(core == 0, 1.0, nearer)
    theirs = jnp.where(core == 0, nearer, 1.0)
    arrived(pr_s, 0)
    for i in range(16):
        ns_s[i // 4, i % 4] = (mine * pl_s[core, i].astype(F32) + theirs * pr_s[i].astype(F32)).astype(BF16)

    def turn(a):
        return lax.rem(res + a + 4, 4)

    across = turn(2)
    send(ns_s.at[pl.ds(0, 2), res], nr_s.at[2, pl.ds(0, 2)], 3, chip_device(z + 2))
    send(ns_s.at[pl.ds(2, 2), res], nr_s.at[2, pl.ds(2, 2)], 4, chip_device(z - 2))
    send(ns_s.at[:, turn(3)], nr_s.at[0], 1, chip_device(z + 1))
    send(ns_s.at[:, turn(1)], nr_s.at[1], 2, chip_device(z - 1))
    bring["tgt"].wait()
    tgt_t[...] = tgt_v[...].astype(F32).T.reshape(tgt_t.shape)

    wait_many(dep, many_recv, 0, 2)
    number = lax.broadcasted_iota(jnp.int32, dep.shape, 0)
    depths = dep[...]

    def light(end):
        return jnp.exp(-jnp.sum(jnp.where(number < end, depths, 0.0), axis=0))

    for i, a in enumerate((0, -1, 1, -2, 2)):
        tt[i] = light(2 * lax.rem(z + a + n_z, n_z))
    tt[5] = light(cell)
    lights = [tt[i, pl.ds(core, 1), :] for i in range(5)]
    arrived(nr_s.at[0], 1)
    arrived(nr_s.at[1], 2)
    arrived(nr_s.at[2, pl.ds(0, 2)], 3)
    arrived(nr_s.at[2, pl.ds(2, 2)], 4)
    for i in range(4):
        fs_s[i] = (
            lights[0] * ns_s[i, across].astype(F32) + lights[1] * nr_s[0, i].astype(F32)
            + lights[2] * nr_s[1, i].astype(F32) + lights[3 + i // 2] * nr_s[2, i].astype(F32)
        ).astype(BF16)
    for a in (6, -6, 2, -2):
        to = lax.rem(z + a + n_z, n_z)
        send_block(fs_s.at[lax.div(to, 4)], fr_s.at[quad], 0, quad, chip_device(to))
    for i in range(4):
        block_arrived(fr_s.at[i], 0, i)
    lit = fr_s[0].astype(F32) + fr_s[1].astype(F32) + fr_s[2].astype(F32) + fr_s[3].astype(F32)

    own_s[...] = (lit - tgt_t[z]).astype(BF16)
    for a in (6, -6, 2, -2):
        send_block(own_s, rs_s.at[core, quad, res], 1, quad, chip_device(z + a + n_z))
    cp_s[...] = lit.reshape(cp_s.shape)
    send(cp_s.at[other], cr_s, 6, sibling)
    for a in (2, -2, 6, -6):
        at = lax.div(lax.rem(z + a + n_z, n_z), 4)
        block = rs_s.at[core, at, across]
        block_arrived(block, 1, at)
        send_block(block, block, 4, at, chip_device(z + 2 + 12 * lax.div(at, 2)))
        send_block(block, block, 2, at, chip_device(z + 1))
        send_block(block, block, 3, at, chip_device(z - 1))
        send_block(block, block, 5, at, sibling)
    sources = ((0, 0), (-1, 1), (1, 2), (-2, 3), (2, 4))
    lit_rows = [0.0] * 5
    for i in range(4):
        block = rs_s[core, i, across].astype(F32)
        for j, piece in ((0, ns_s[i, across]), (1, nr_s[0, i]), (2, nr_s[1, i]), (3 + i // 2, nr_s[2, i])):
            lit_rows[j] = lit_rows[j] + block * piece.astype(F32)
    chip = lax.broadcasted_iota(jnp.int32, (n_z, HALF), 0)
    behind = jnp.zeros((n_z, HALF), F32)
    for a, j in sources:
        row = lights[j] * jnp.sum(lit_rows[j], axis=0, keepdims=True)
        behind = behind + jnp.where(chip < lax.rem(z + a + n_z, n_z), row, 0.0)
    for i in range(n_z):
        pb[i] = behind[i:i + 1]

    def to_chip(j, n):
        to = lax.rem(z + away(j, n_z), n_z)
        pltpu.make_async_remote_copy(
            pb.at[to], rb.at[z], many_send.at[1], many_recv.at[1],
            device_id=(to, core, y, x), device_id_type=MESH).start()
        return n

    lax.fori_loop(0, n_z - 1, to_chip, 0)
    rb[z] = pb[z]

    for a in (2, -2, 6, -6):
        for i, beside, which in ((2, -1, turn(1)), (3, 1, turn(3)), (4, 2, res)):
            at = lax.div(lax.rem(z + beside + a + n_z, n_z), 4)
            block = rs_s.at[core, at, which]
            block_arrived(block, i, at)
            send_block(block, block, 4 + i, at, sibling)
    for i, which in ((5, across), (6, turn(1)), (7, turn(3)), (8, res)):
        for at in range(4):
            block_arrived(rs_s.at[other, at, which], i, at)

    transmit = tt[5]
    for half in range(2):
        block = rs_s[half].reshape(gp.shape[0], HALF).astype(F32)
        gp[:, half * HALF:(half + 1) * HALF] = (block * transmit[half:half + 1]).astype(BF16)
    q_t[...] = mm(wfb[...], gp[...])
    slopes = []
    for k in range(SAMPLES):
        slopes.append(jnp.sum(h2[k].astype(F32) * q_t[...], axis=0, keepdims=True))
    slope = jnp.concatenate(slopes, axis=0)
    lit_slope = weight * slope
    put_rows(br, core, jnp.sum(lit_slope, axis=0, keepdims=True))
    send(br.at[core], br.at[core], 7, sibling)
    wait_many(rb, many_recv, 1, 1)
    lp[core] = jnp.sum(rb[...], axis=0)
    send(lp.at[core], lp.at[core], 9, sibling)
    gf_s[...] = nt_dot(gathered, gp[...]).astype(BF16).reshape(gf_s.shape)
    to_groups(lambda t: gf_s.at[t], gf_r, 2)

    arrived(cr_s, 6)
    first_half = jnp.where(core == 0, cp_s[core], cr_s[...])
    second_half = jnp.where(core == 0, cr_s[...], cp_s[core])
    ren_o[...] = jnp.concatenate([first_half, second_half], axis=1).astype(BF16)
    gf_r[group] = gf_s[group]
    after = jnp.sum(lit_slope, axis=0, keepdims=True) - ahead_of(lit_slope) - lit_slope
    slope_step = slope * (ahead * kept) - after
    slope_scale = travel / (1.0 + jnp.exp(-logit))

    arrived(br.at[other], 7)
    follower = jnp.where(core == 0, br[1], 0.0)
    arrived(lp.at[other], 9)
    grad_depth = -jnp.concatenate([lp[0] + follower[0:1], lp[1] + follower[1:2]], axis=1)
    dg_o[...] = grad_depth
    grad_logit = (grad_depth + slope_step) * slope_scale
    for k in range(SAMPLES):
        grad = weight[k:k + 1] * q_t[...] + grad_logit[k:k + 1] * wdb[...]
        gb[:, k * n_rows:(k + 1) * n_rows] = jnp.where(h2[k].astype(F32) > 0.0, grad, 0.0).astype(BF16)
    gs_s[...] = nt_dot(h1[...], gb[...]).astype(BF16).reshape(gs_s.shape)
    to_groups(lambda t: gs_s.at[t], gs_r, 3)
    gs_r[group] = gs_s[group]

    def folded(share):
        squares = jnp.sum(share * share, axis=0, keepdims=True)
        return sum(squares[:, i:i + HALF] for i in range(0, squares.shape[1], HALF))

    wait_many(gf_r, many_recv, 2, 1)
    share_feature = jnp.sum(gf_r[...].astype(F32), axis=0)
    square_feature = folded(share_feature)
    fa_s[...] = share_feature.astype(BF16)
    to_groups(lambda t: fa_s, gf_o, 5)
    own_feature = pltpu.make_async_copy(fa_s, gf_o.at[group], loc.at[10])
    own_feature.start()
    wait_many(gs_r, many_recv, 3, 1)
    share_second = jnp.sum(gs_r[...].astype(F32), axis=0)
    sq[cell] = square_feature + folded(share_second)
    send(sq.at[cell], sq.at[cell], 8, sibling)
    to_cells(sq, 4)
    sa_s[...] = share_second.astype(BF16)
    to_groups(lambda t: sa_s, gs_o, 6)
    own_second = pltpu.make_async_copy(sa_s, gs_o.at[group], loc.at[11])
    own_second.start()
    arrived(sq.at[2 * z + other], 8)
    wait_many(sq, many_recv, 4, 2)
    sr[group] = jnp.sum(sq[...], axis=0)
    to_groups(lambda t: sr.at[group], sr, 7)
    wait_many(gf_o, many_recv, 5, 1)
    wait_many(gs_o, many_recv, 6, 1)
    own_feature.wait()
    own_second.wait()
    for copy in sent:
        copy.wait_send()
    for i, (buf, left_out) in enumerate((
        (dep, 2), (rb, 1), (gf_r, 1), (gs_r, 1), (sq, 2), (gf_o, 1), (gs_o, 1), (sr, 1),
    )):
        wait_many(buf, many_send, i, left_out)
    wait_many(sr, many_recv, 7, 1)
    sum_o[...] = jnp.sum(sr[...], axis=0)


def adam_kernel(
    entries,
    ren_h, dg_h, gs_h, gf_h, sum_h, ms_h, vs_h, mf_h, vf_h,
    ren_o, dg_o, us_o, uf_o,
    gs_v, gf_v, sum_v, ms_v, vs_v, mf_v, vf_v, us_v, uf_v,
    sem, feed, drain,
):
    n_rays, per, _ = gs_v.shape
    parts = feed.shape[0]
    groups, rows = n_rays // parts, per * n_rays // parts
    start = []
    for i, (src, dst) in enumerate(((sum_h, sum_v), (ren_h, ren_o), (dg_h, dg_o))):
        copy = pltpu.make_async_copy(src, dst, sem.at[i])
        copy.start()
        start.append(copy)
    fed = []
    for i in range(parts):
        some, block = pl.ds(i * rows, rows), pl.ds(i * groups, groups)
        copies = [
            pltpu.make_async_copy(gs_h.at[block], gs_v.at[block], feed.at[i, 0]),
            pltpu.make_async_copy(gf_h.at[block], gf_v.at[block], feed.at[i, 5]),
        ]
        for j, (src, dst) in enumerate(((ms_h, ms_v), (vs_h, vs_v), (mf_h, mf_v), (vf_h, vf_v))):
            copies.append(pltpu.make_async_copy(src.at[some], dst.at[some], feed.at[i, 1 + j]))
        for copy in copies:
            copy.start()
        fed.append(copies)
    start[0].wait()
    square_sum = jnp.sum(sum_v[...], axis=1, keepdims=True)
    rescale = lax.rsqrt(square_sum / entries + mean_floor)

    def adam(gradient, mean_moment, square_moment):
        unit = gradient.astype(F32) * rescale
        mean_new = beta_first * mean_moment + (1.0 - beta_first) * unit
        square_new = beta_second * square_moment + (1.0 - beta_second) * unit * unit
        spread = square_new * (1.0 / bias_second)
        spread = spread * lax.rsqrt(spread) + adam_floor
        return (mean_new * (1.0 / bias_first) * pltpu.reciprocal(spread)).astype(BF16)

    def update(i, n):
        at = pl.ds(pl.multiple_of(i * per, per), per)
        us_v[at, :] = adam(gs_v[i], ms_v[at, :], vs_v[at, :])
        uf_v[at, :] = adam(gf_v[i], mf_v[at, :], vf_v[at, :])
        return n

    out = []
    for i in range(parts):
        for copy in fed[i]:
            copy.wait()
        lax.fori_loop(i * groups, (i + 1) * groups, update, 0)
        some = pl.ds(i * rows, rows)
        for j, (src, dst) in enumerate(((us_v, us_o), (uf_v, uf_o))):
            out.append(pltpu.make_async_copy(src.at[some], dst.at[some], drain.at[i, j]))
            out[-1].start()
    for copy in out + start[1:]:
        copy.wait()


def on_device(sizes, ray_code, entry_index, sample_count, step_length, positions, w_first, w_second,
              w_density, w_feature, mean_second, square_second, mean_feature, square_feature, target_color):
    n_z, n_y, n_x, all_cells = sizes
    n_cell, n_rays = 2 * n_z, n_y * n_x
    rows, width = ray_code.shape[0], ray_code.shape[2]
    table, channels = positions.shape[1], target_color.shape[1]
    part = channels // 16
    per = width // n_rays
    vmem = pltpu.VMEM
    args = (
        ray_code.reshape(rows, width), entry_index.reshape(1, rows), sample_count.reshape(1, rows),
        step_length.reshape(1, rows), positions[0], w_first[0], w_second[0], w_density,
        w_feature[0], target_color,
    )
    moments = (mean_second[0], square_second[0], mean_feature[0], square_feature[0])
    local = [vmem(a.shape, a.dtype) for a in args[:-1]] + [vmem((HALF, channels), BF16)]
    scratch = local + [
        vmem((width, rows), F32), vmem((width, 2 * table), BF16),
        vmem((width, width), BF16), vmem((channels, width), BF16), vmem((width, channels), BF16),
        vmem((width, rows), F32), vmem((width, SAMPLES * rows), BF16), vmem((SAMPLES, width, rows), BF16),
        vmem((SAMPLES, rows), F32), vmem((16, part, HALF), F32), vmem((width, rows), F32),
        vmem((channels, rows), BF16), vmem((width, SAMPLES * rows), BF16),
        vmem((n_cell, 2, HALF), F32), vmem((6, 2, HALF), F32), vmem((2, 16, part, HALF), BF16),
        vmem((16, part, HALF), BF16), vmem((4, 4, part, HALF), BF16), vmem((3, 4, part, HALF), BF16),
        vmem((4, part, HALF), BF16), vmem((4, part, HALF), BF16), vmem((2, part // 2, HALF), F32),
        vmem((part // 2, HALF), F32), vmem((part, HALF), BF16), vmem((2, 4, 4, part, HALF), BF16), vmem((2, 2, HALF), F32),
        vmem((n_z, 1, HALF), F32), vmem((n_z, 1, HALF), F32), vmem((2, 1, HALF), F32),
        vmem((n_rays, per, channels), BF16), vmem((n_rays, per, channels), BF16),
        vmem((n_rays, per, width), BF16), vmem((n_rays, per, width), BF16),
        vmem((per, channels), BF16), vmem((per, width), BF16), vmem((n_cell, 1, HALF), F32), vmem((n_rays, 1, HALF), F32),
        pltpu.SemaphoreType.DMA((12,)), pltpu.SemaphoreType.DMA((8,)), pltpu.SemaphoreType.DMA((8,)),
        pltpu.SemaphoreType.DMA((10,)), pltpu.SemaphoreType.DMA((10,)),
        pltpu.SemaphoreType.DMA((36,)), pltpu.SemaphoreType.DMA((9, 4)),
    ]
    anywhere = pl.BlockSpec(memory_space=pl.ANY)
    inside = pl.BlockSpec(memory_space=vmem)
    found = pl.pallas_call(
        functools.partial(kernel, sizes),
        out_shape=(
            jax.ShapeDtypeStruct((part // 2, rows), BF16),
            jax.ShapeDtypeStruct((1, rows), F32),
            jax.ShapeDtypeStruct((n_rays, per, width), BF16),
            jax.ShapeDtypeStruct((n_rays, per, channels), BF16),
            jax.ShapeDtypeStruct((1, HALF), F32),
        ),
        in_specs=[anywhere] * len(args),
        out_specs=[inside, inside, anywhere, anywhere, inside],
        scratch_shapes=scratch,
        compiler_params=pltpu.CompilerParams(
            collective_id=0, has_side_effects=True, vmem_limit_bytes=62 * 1024 * 1024
        ),
    )(*args)
    parts = min(4, n_rays)
    rendered, depth_grad, update_second, update_feature = pl.pallas_call(
        functools.partial(adam_kernel, all_cells * width * (width + channels)),
        out_shape=(
            jax.ShapeDtypeStruct((part // 2, rows), BF16),
            jax.ShapeDtypeStruct((1, rows), F32),
            jax.ShapeDtypeStruct((width, width), BF16),
            jax.ShapeDtypeStruct((width, channels), BF16),
        ),
        in_specs=[anywhere] * 9,
        out_specs=[anywhere] * 4,
        scratch_shapes=[
            vmem((n_rays, per, width), BF16), vmem((n_rays, per, channels), BF16), vmem((1, HALF), F32),
            *(vmem(m.shape, F32) for m in moments),
            vmem((width, width), BF16), vmem((width, channels), BF16),
            pltpu.SemaphoreType.DMA((3,)), pltpu.SemaphoreType.DMA((parts, 6)), pltpu.SemaphoreType.DMA((parts, 2)),
        ],
        compiler_params=pltpu.CompilerParams(vmem_limit_bytes=62 * 1024 * 1024),
    )(*found, *moments)
    return (rendered.T, depth_grad.reshape(rows, 1), update_second[None], update_feature[None])


def solution(mesh):
    n_cell, n_rays = mesh.devices.shape
    n_y = 4 if n_rays == 16 else 1
    sizes = (n_cell // 2, n_y, n_rays // n_y, n_cell)
    split = Mesh(mesh.devices.reshape(n_cell // 2, 2, n_y, n_rays // n_y), ("z", "core", "y", "x"))
    return jax.shard_map(
        functools.partial(on_device, sizes),
        mesh=split,
        in_specs=(
            P(RAYS, CELL, None),
            P(RAYS, CELL),
            P(RAYS, CELL),
            P(RAYS, CELL),
            P(CELL, None, None),
            P(CELL, None, None),
            P(CELL, None, None),
            P(CELL, None),
            P(CELL, None, None),
            P(CELL, None, None),
            P(CELL, None, None),
            P(CELL, None, None),
            P(CELL, None, None),
            P(RAYS, None),
        ),
        out_specs=(P(RAYS, CELL), P(RAYS, CELL), P(CELL, None, None), P(CELL, None, None)),
        check_vma=False,
    )
```
